512 devices in a mesh: dp: 32 (over y, x), seq: 16 (over z, core).
Axes of the slice: x: 4, y: 8, z: 8, core: 2. Of those that a mesh axis runs over, the one named last changes fastest.
Arguments:
- queries: bfloat16 [65536, 6144], P(('dp', 'seq')), may hold values from -5 to 5
- keys: bfloat16 [65536, 512], P(('dp', 'seq')), may hold values from -5 to 5
- values: bfloat16 [65536, 512], P(('dp', 'seq')), may hold values from -5 to 5
- grad_out: bfloat16 [65536, 6144], P(('dp', 'seq')), may hold values from -5 to 5
- prefix_keys: bfloat16 [384, 512], P('seq'), may hold values from -5 to 5
- prefix_values: bfloat16 [384, 512], P('seq'), may hold values from -5 to 5
- doc_lengths: int32 [32, 8], P('dp'), may hold values from 1 to 512, 2048 in all within a row
- doc_tenants: int32 [32, 8], P('dp'), may hold values from 0 to 5
- tenant_slots: int32 [6], replicated, may hold values from 0 to 5, each once
Outputs:
- grad_keys: bfloat16 [65536, 512], P(('dp', 'seq'))
- grad_values: bfloat16 [65536, 512], P(('dp', 'seq'))
- prefix_key_grads: float32 [384, 512], P('seq')
- prefix_value_grads: float32 [384, 512], P('seq')
The draws below stay inside these ranges and needn't reach their ends.
Inputs may be any that keep to these rules, and one draw needn't show every extreme that they name: `doc_lengths`: each row sums to 2048; its largest entry is exactly 512. `tenant_slots`: each slot once.
All inputs are finite; a program needn't handle non-finite values.
Results may differ from the reference program's by a relative error of at most 0.0058.
Values may be sent and summed in bfloat16 or wider, within the bound.
No kernel may reach another device: no remote copies, remote signals or barrier semaphores. Data moves between devices by JAX's collectives and lax.ppermute only.
A program may use at most 64 MiB of HBM per device.

```python
import math
import jax
import jax.numpy as jnp
import numpy as np
from jax import lax

HQ = 48
KVH = 4
HD = 128
PLEN = 64
TENANTS = 6
QBLK = 256
SEQ_LEN = 2048
GROUPS = 32
TOKENS = 65536
DOC_MOST = 512
DOCS = 8
PREF_ROWS = 384
N_DP = 32
N_SEQ = 16


def shared_keys(key):
    return jax.random.truncated_normal(key, -5.0, 5.0, (TOKENS, KVH, HD), jnp.float32)


def draw_keys(key, part):
    base_keys = shared_keys(key)
    return base_keys.reshape(TOKENS, KVH * HD).astype(jnp.bfloat16)


def draw_queries(key, part):
    key = jax.random.fold_in(key, 5)
    drawn_rows = jax.random.truncated_normal(key, -5.0, 5.0, (TOKENS, HQ, HD), jnp.float32)
    return drawn_rows.reshape(TOKENS, HQ * HD).astype(jnp.bfloat16)


def set_ends(values, stream_key, smallest, largest):
    dims = values.shape
    spot = [jax.random.randint(jax.random.fold_in(stream_key, axis), (), 0, dims[axis]) for axis in range(len(dims))]
    values = values.at[tuple(spot)].set(smallest)
    longest = dims.index(max(dims))
    spot[longest] = (spot[longest] + 1) % dims[longest]
    return values.at[tuple(spot)].set(largest)


def shard_levels(stream_key, extent, cuts, least, top_value):
    def one(axis_at, shards_of):
        steps = jax.random.uniform(jax.random.fold_in(jax.random.fold_in(stream_key, 6), axis_at), (shards_of,), jnp.float32, least / len(cuts), top_value / len(cuts))
        return jnp.repeat(jnp.exp(steps), extent[axis_at] // shards_of).reshape((-1,) + (1,) * (len(extent) - axis_at - 1))

    level = one(*cuts[0])
    for cut in cuts[1:]:
        level = level * one(*cut)
    return level


def length_profile(count, total, bound, skew):
    portions = [(1 << 20) // math.isqrt(grade ** skew) + 1 for grade in range(2, count + 1)]
    surplus, counts = total - bound - (count - 1), [1] * (count - 1)
    while surplus > 0:
        candidates = [i for i in range(count - 1) if counts[i] < bound]
        whole, budget = sum([portions[i] for i in candidates]), surplus
        for i in candidates:
            extra = min(bound - counts[i], max(1, budget * portions[i] // whole), surplus)
            counts[i] = counts[i] + extra
            surplus = surplus - extra
    return np.array([bound] + counts)


def ragged(own_key, amount, total, reach, lean):
    if amount == 2:
        one = jax.random.randint(own_key, (), max(1, total - reach), min(reach, total - 1) + 1)
        return jnp.stack([one, total - one])
    sizes = jnp.asarray(length_profile(amount, total, reach, lean), jnp.int32)
    twos = (amount - 1) // 2
    source_of, receiver = sizes[1:1 + 2 * twos:2], sizes[2:2 + 2 * twos:2]
    room = jnp.minimum(source_of - 1, reach - receiver)
    moved = jax.random.randint(jax.random.fold_in(own_key, 1), (twos,), 0, 1 << 20) % (room + 1)
    sizes = sizes.at[1:1 + 2 * twos:2].set(source_of - moved).at[2:2 + 2 * twos:2].set(receiver + moved)
    return sizes[jax.random.permutation(jax.random.fold_in(own_key, 2), amount)]


def scatter_about(stream_key, extent, spread, limit, split=(), kind=jnp.bfloat16):
    entries = spread * jax.random.normal(stream_key, extent, jnp.float32)
    if split:
        entries = entries * shard_levels(stream_key, extent, split, -0.22, 0.18)
    return jnp.clip(entries, -limit, limit).astype(kind)


def setup_inputs(seed: int = 0) -> dict:
    seeds = jax.random.split(jax.random.key(seed), 10)
    return {
        "queries": draw_queries(jax.random.fold_in(seeds[9], 71), 0),
        "keys": draw_keys(jax.random.fold_in(seeds[9], 71), 0),
        "values": scatter_about(seeds[2], (TOKENS, KVH * HD), 1.0, 5.0, ((0, 512),)),
        "grad_out": scatter_about(seeds[3], (TOKENS, HQ * HD), 1.0, 5.0, ((0, 512),)),
        "prefix_keys": scatter_about(seeds[4], (PREF_ROWS, KVH * HD), 1.0, 5.0, ((0, 16),)),
        "prefix_values": scatter_about(seeds[5], (PREF_ROWS, KVH * HD), 1.0, 5.0, ((0, 16),)),
        "doc_lengths": jax.vmap(lambda own: ragged(own, DOCS, SEQ_LEN, DOC_MOST, 1))(jax.random.split(seeds[6], GROUPS)).reshape((GROUPS, DOCS)).astype(jnp.int32),
        "doc_tenants": set_ends(jax.random.randint(seeds[7], (GROUPS, DOCS), 0, TENANTS), jax.random.fold_in(seeds[7], 1), 0, TENANTS - 1).astype(jnp.int32),
        "tenant_slots": jax.random.permutation(seeds[8], TENANTS).astype(jnp.int32),
    }


def token_layout(lengths, tenants, slots, seq_len):
    doc_ends = jnp.cumsum(lengths).astype(jnp.int32)
    positions = jnp.arange(seq_len, dtype=jnp.int32)
    doc_of = lax.optimization_barrier(jnp.sum((positions[:, None] >= doc_ends[None, :]).astype(jnp.int32), axis=1))
    tenant_range = jnp.arange(slots.shape[0], dtype=jnp.int32)
    doc_slot = lax.optimization_barrier(jnp.sum(jnp.where(tenants[:, None] == tenant_range[None, :], slots[None, :], 0), axis=1))
    doc_range = jnp.arange(lengths.shape[0], dtype=jnp.int32)
    token_slot = lax.optimization_barrier(jnp.sum(jnp.where(doc_of[:, None] == doc_range[None, :], doc_slot[None, :], 0), axis=1))
    return (doc_of.astype(jnp.int32), token_slot.astype(jnp.int32))

def rounded(tensor):
    return lax.optimization_barrier(tensor.astype(jnp.bfloat16)).astype(jnp.float32)

def block_grads(query_blk, grad_blk, keys_all, values_all, allowed, inv_root, runs):
    query_f = query_blk.astype(jnp.float32)
    grad_f = grad_blk.astype(jnp.float32)
    scores = jnp.einsum('qhd,kd->hqk', query_f, keys_all.astype(jnp.float32)) * inv_root
    scores = jnp.where(allowed[None], scores, jnp.float32(-1e+30))
    row_max = lax.optimization_barrier(jnp.max(scores, axis=-1, keepdims=True))
    probs = jnp.exp(scores - row_max)
    probs = probs / lax.optimization_barrier(jnp.sum(probs, axis=-1, keepdims=True))
    probs_b = rounded(probs)
    grad_probs = jnp.einsum('qhd,kd->hqk', grad_f, values_all.astype(jnp.float32))
    row_delta = lax.optimization_barrier(jnp.sum(probs * grad_probs, axis=-1, keepdims=True))
    grad_scores = rounded(probs * (grad_probs - row_delta))
    heads, rows, cols = grad_scores.shape
    per_run = heads // runs
    query_r = query_f.reshape(rows, runs, per_run, query_f.shape[-1])
    grad_r = grad_f.reshape(rows, runs, per_run, grad_f.shape[-1])
    key_grad = jnp.einsum('rsqk,qrsd->rkd', grad_scores.reshape(runs, per_run, rows, cols), query_r) * inv_root
    value_grad = jnp.einsum('rsqk,qrsd->rkd', probs_b.reshape(runs, per_run, rows, cols), grad_r)
    return (key_grad, value_grad)

def reference(queries, keys, values, grad_out, prefix_keys, prefix_values, doc_lengths, doc_tenants, tenant_slots):
    group_size = HQ // KVH
    runs = N_SEQ // KVH
    inv_root = 1.0 / math.sqrt(HD)
    window = DOC_MOST + QBLK
    pref_slot = jnp.arange(PREF_ROWS, dtype=jnp.int32) // PLEN
    query_all = queries.reshape(N_DP, SEQ_LEN, KVH, group_size, HD).transpose(0, 2, 1, 3, 4)
    grad_all = grad_out.reshape(N_DP, SEQ_LEN, KVH, group_size, HD).transpose(0, 2, 1, 3, 4)
    key_all = keys.reshape(N_DP, SEQ_LEN, KVH, HD).transpose(0, 2, 1, 3)
    value_all = values.reshape(N_DP, SEQ_LEN, KVH, HD).transpose(0, 2, 1, 3)
    pkey_heads = prefix_keys.reshape(PREF_ROWS, KVH, HD).transpose(1, 0, 2)
    pvalue_heads = prefix_values.reshape(PREF_ROWS, KVH, HD).transpose(1, 0, 2)

    def one_group(inputs):
        query_grp, grad_grp, key_grp, value_grp, lengths, tenants = inputs
        doc_of, token_slot = token_layout(lengths, tenants, tenant_slots, SEQ_LEN)
        doc_pad = jnp.concatenate([jnp.full((DOC_MOST,), -1, jnp.int32), doc_of])

        def one_head(head_inputs):
            query_head, grad_head, key_head, value_head, pkey_head, pvalue_head = head_inputs
            zero_rows = jnp.zeros((DOC_MOST, HD), key_head.dtype)
            key_pad = jnp.concatenate([zero_rows, key_head], axis=0)
            value_pad = jnp.concatenate([zero_rows, value_head], axis=0)

            def block_step(block_index, carried):
                dkey_pad, dvalue_pad, dkey_pref, dvalue_pref = carried
                row_start = jnp.asarray(block_index * QBLK).astype(jnp.int32)
                query_blk = lax.dynamic_slice_in_dim(query_head, row_start, QBLK, 0)
                grad_blk = lax.dynamic_slice_in_dim(grad_head, row_start, QBLK, 0)
                key_win = lax.dynamic_slice_in_dim(key_pad, row_start, window, 0)
                value_win = lax.dynamic_slice_in_dim(value_pad, row_start, window, 0)
                doc_win = lax.dynamic_slice_in_dim(doc_pad, row_start, window, 0)
                key_pos = row_start - DOC_MOST + jnp.arange(window, dtype=jnp.int32)
                query_doc = lax.dynamic_slice_in_dim(doc_of, row_start, QBLK, 0)
                query_slot = lax.dynamic_slice_in_dim(token_slot, row_start, QBLK, 0)
                query_pos = row_start + jnp.arange(QBLK, dtype=jnp.int32)
                token_allowed = (doc_win[None, :] == query_doc[:, None]) & (key_pos[None, :] <= query_pos[:, None])
                prefix_allowed = pref_slot[None, :] == query_slot[:, None]
                allowed = jnp.concatenate([token_allowed, prefix_allowed], axis=1)
                keys_cat = jnp.concatenate([key_win, pkey_head], axis=0)
                values_cat = jnp.concatenate([value_win, pvalue_head], axis=0)
                key_grad, value_grad = block_grads(query_blk, grad_blk, keys_cat, values_cat, allowed, inv_root, runs)
                old_keys = lax.dynamic_slice_in_dim(dkey_pad, row_start, window, 1)
                old_values = lax.dynamic_slice_in_dim(dvalue_pad, row_start, window, 1)
                dkey_pad = lax.dynamic_update_slice_in_dim(dkey_pad, old_keys + key_grad[:, :window], row_start, 1)
                dvalue_pad = lax.dynamic_update_slice_in_dim(dvalue_pad, old_values + value_grad[:, :window], row_start, 1)
                return (dkey_pad, dvalue_pad, dkey_pref + key_grad[:, window:], dvalue_pref + value_grad[:, window:])
            zero_pad = jnp.zeros((runs, DOC_MOST + SEQ_LEN, HD), jnp.float32)
            zero_pref = jnp.zeros((runs, PREF_ROWS, HD), jnp.float32)
            dkey_pad, dvalue_pad, dkey_pref, dvalue_pref = lax.fori_loop(0, SEQ_LEN // QBLK, block_step, (zero_pad, zero_pad, zero_pref, zero_pref))
            dkey_tok = lax.optimization_barrier(jnp.sum(rounded(dkey_pad[:, DOC_MOST:]), axis=0))
            dvalue_tok = lax.optimization_barrier(jnp.sum(rounded(dvalue_pad[:, DOC_MOST:]), axis=0))
            return (dkey_tok, dvalue_tok, lax.optimization_barrier(jnp.sum(dkey_pref, axis=0)), lax.optimization_barrier(jnp.sum(dvalue_pref, axis=0)))
        return lax.map(one_head, (query_grp, grad_grp, key_grp, value_grp, pkey_heads, pvalue_heads))
    dkey_all, dvalue_all, dkey_pref, dvalue_pref = lax.map(one_group, (query_all, grad_all, key_all, value_all, doc_lengths, doc_tenants))
    grad_keys = dkey_all.transpose(0, 2, 1, 3).reshape(N_DP * SEQ_LEN, KVH * HD).astype(jnp.bfloat16)
    grad_values = dvalue_all.transpose(0, 2, 1, 3).reshape(N_DP * SEQ_LEN, KVH * HD).astype(jnp.bfloat16)
    prefix_key_grads = lax.optimization_barrier(jnp.sum(dkey_pref, axis=0)).transpose(1, 0, 2).reshape(PREF_ROWS, KVH * HD)
    prefix_value_grads = lax.optimization_barrier(jnp.sum(dvalue_pref, axis=0)).transpose(1, 0, 2).reshape(PREF_ROWS, KVH * HD)
    return (grad_keys, grad_values, prefix_key_grads, prefix_value_grads)
```

```python
import functools
import math

import jax
import jax.numpy as jnp
from jax import lax
from jax.experimental import pallas as pl
from jax.experimental.pallas import tpu as pltpu
from jax.sharding import Mesh, PartitionSpec as P

HQ = 48
KVH = 4
HD = 128
PLEN = 64
DOC_MOST = 512
SEQ = ("z", "core")
DP = ("y", "x")
NT = (((1,), (1,)), ((), ()))
NN = (((1,), (0,)), ((), ()))


def grads_kernel(per, q_ref, g_ref, *refs):
    k_refs, v_refs, (pk_ref, pv_ref, bias_ref) = refs[:5], refs[5:10], refs[10:13]
    near_k, near_v, far_k, far_v, pref_ref = refs[13:]
    heads = q_ref.shape[1] // HD
    toks = q_ref.shape[0]
    scale = 1.0 / math.sqrt(HD)
    log2e = scale * math.log2(math.e)
    keys = jnp.concatenate([r[...] for r in k_refs] + [pk_ref[...]], axis=0)
    values = jnp.concatenate([r[...] for r in v_refs] + [pv_ref[...]], axis=0)
    rows = keys.shape[0]
    bias = jnp.concatenate([bias_ref[...]] * per, axis=1)

    def step(i, sums):
        dk, dv = sums
        cols = [pl.ds(pl.multiple_of((i * per + j) * HD, HD), HD) for j in range(per)]
        q = jnp.concatenate([q_ref[:, c] for c in cols], axis=0)
        g = jnp.concatenate([g_ref[:, c] for c in cols], axis=0)
        s = lax.dot_general(keys, q, NT, preferred_element_type=jnp.float32) + bias
        dp = lax.dot_general(values, g, NT, preferred_element_type=jnp.float32)
        top = jnp.max(s, axis=0, keepdims=True) * log2e
        e = jnp.exp2(s * log2e - top)
        inv = 1.0 / jnp.sum(e, axis=0, keepdims=True)
        delta = jnp.sum(e * dp, axis=0, keepdims=True) * inv
        p = e * inv
        ds = (p * (dp - delta)).astype(jnp.bfloat16)
        dk = dk + lax.dot_general(ds, q, NN, preferred_element_type=jnp.float32)
        dv = dv + lax.dot_general(
            p.astype(jnp.bfloat16), g, NN, preferred_element_type=jnp.float32
        )
        return dk, dv

    zero = jnp.zeros((rows, HD), jnp.float32)
    dk, dv = lax.fori_loop(0, heads // per, step, (zero, zero))
    dk = dk * scale
    near = 3 * toks
    win = 5 * toks
    near_k[...] = dk[:near]
    near_v[...] = dv[:near]
    far_k[...] = dk[near:win].astype(jnp.bfloat16)
    far_v[...] = dv[near:win].astype(jnp.bfloat16)
    halves, parts, both, _ = pref_ref.shape
    each = both // 2
    for half in range(halves):
        for part in range(parts):
            at = win + (part * halves + half) * each
            pref_ref[half, part, :each, :] = dk[at : at + each]
            pref_ref[half, part, each:, :] = dv[at : at + each]


def grads(q, g, blocks, pref, bias, halves, parts, per=2):
    toks, width = q.shape
    prefs = pref.shape[0]
    both = 2 * prefs // (halves * parts)
    run = width // KVH

    def cols(rows, wide, shift=0):
        return pl.BlockSpec((rows, wide), lambda h: (0, h + shift))

    return pl.pallas_call(
        functools.partial(grads_kernel, per),
        grid=(KVH,),
        in_specs=[cols(toks, run)] * 2
        + [cols(toks, HD)] * 5
        + [cols(toks, HD, KVH)] * 5
        + [cols(prefs, HD), cols(prefs, HD, KVH)]
        + [pl.BlockSpec(bias.shape, lambda h: (0, 0))],
        out_specs=[cols(3 * toks, HD)] * 2
        + [cols(2 * toks, HD)] * 2
        + [pl.BlockSpec((halves, parts, both, HD), lambda h: (0, 0, 0, h))],
        out_shape=[jax.ShapeDtypeStruct((3 * toks, KVH * HD), jnp.float32)] * 2
        + [jax.ShapeDtypeStruct((2 * toks, KVH * HD), jnp.bfloat16)] * 2
        + [jax.ShapeDtypeStruct((halves, parts, both, KVH * HD), jnp.float32)],
        compiler_params=pltpu.CompilerParams(vmem_limit_bytes=56 << 20),
        cost_estimate=pl.CostEstimate(
            flops=8 * toks * width * bias.shape[0],
            bytes_accessed=10 << 20,
            transcendentals=toks * width // HD * bias.shape[0],
        ),
    )(q, g, *blocks, *blocks, pref, pref, bias)


def visible_bias(lengths, tenants, slots, index, shards, toks, prefs):
    ends = jnp.cumsum(lengths)
    slot_of = jnp.sum(
        jnp.where(tenants[:, None] == jnp.arange(slots.shape[0])[None, :], slots[None, :], 0), axis=1
    )
    here = index * toks + jnp.arange(toks, dtype=jnp.int32)
    doc = jnp.sum((here[None, :] >= ends[:, None]).astype(jnp.int32), axis=0)
    starts = ends - lengths
    pick = doc[None, :] == jnp.arange(lengths.shape[0])[:, None]
    first = jnp.sum(jnp.where(pick, starts[:, None], 0), axis=0)
    slot = jnp.sum(jnp.where(pick, slot_of[:, None], 0), axis=0)
    key = jnp.concatenate([s * toks + jnp.arange(toks, dtype=jnp.int32) for s in shards])
    token_ok = (key[:, None] >= first[None, :]) & (key[:, None] <= here[None, :])
    pref_ok = (jnp.arange(prefs, dtype=jnp.int32) // PLEN)[:, None] == slot[None, :]
    ok = jnp.concatenate([token_ok, pref_ok], axis=0)
    return jnp.where(ok, 0.0, -1e30).astype(jnp.float32)


def per_device(
    queries, keys, values, grad_out, prefix_keys, prefix_values, doc_lengths, doc_tenants, tenant_slots
):
    toks = queries.shape[0]
    parts, halves = lax.axis_size("z"), lax.axis_size("core")
    count = parts * halves
    copies = lax.axis_size("y") * lax.axis_size("x")
    index, core = lax.axis_index(SEQ), lax.axis_index("core")

    def shift(x, steps):
        pairs = [(i, i + 2 * steps) for i in range(count) if 0 <= i + 2 * steps < count]
        return lax.ppermute(x, SEQ, pairs)

    def swap(x):
        return lax.ppermute(x, SEQ, [(i, i ^ 1) for i in range(count)])

    own = jnp.concatenate([keys, values], axis=1)
    back1, back2 = shift(own, 1), shift(own, 2)
    pref = lax.all_gather(
        jnp.concatenate([prefix_keys, prefix_values], axis=1), SEQ, axis=0, tiled=True
    )
    cross1 = swap(back1)
    cross02 = swap(jnp.where(core == 0, own, back2))
    even = core == 0
    shards = [
        index - 4,
        index - 2,
        index,
        jnp.where(even, index - 3, index - 1),
        jnp.where(even, index - 1, index - 3),
    ]
    bias = visible_bias(
        doc_lengths[0], doc_tenants[0], tenant_slots, index, shards, toks, pref.shape[0]
    )
    near_k, near_v, far_k, far_v, dpref = grads(
        queries, grad_out, (back2, back1, own, cross02, cross1), pref, bias, halves, parts
    )

    other = swap(jnp.where(even, dpref[1], dpref[0]))
    mine = jnp.where(even, dpref[0], dpref[1]) + other
    got = lax.all_to_all(mine.astype(jnp.bfloat16), "z", split_axis=0, concat_axis=0, tiled=True)
    summed = jnp.sum(got.astype(jnp.float32), axis=0)
    pieces = summed.reshape(copies, -1, HD)
    got = lax.all_to_all(pieces, DP, split_axis=0, concat_axis=0, tiled=True)
    piece = jnp.sum(got, axis=0)
    spread = jnp.broadcast_to(piece[None], pieces.shape)
    full = lax.all_to_all(spread, DP, split_axis=0, concat_axis=0, tiled=True)
    full = full.reshape(summed.shape)
    each = prefix_keys.shape[0]

    far = swap(jnp.concatenate([far_k, far_v], axis=1)).astype(jnp.float32)
    near = jnp.concatenate([near_k, near_v], axis=1)
    zero = jnp.zeros((toks, far.shape[1]), jnp.float32)
    two = near[:toks] + jnp.where(even, zero, far[:toks])
    one = near[toks : 2 * toks] + far[toks:]
    home = near[2 * toks :] + jnp.where(even, far[:toks], zero)
    one = shift(one.astype(jnp.bfloat16), -1)
    two = shift(two.astype(jnp.bfloat16), -2)
    total = (home + one.astype(jnp.float32) + two.astype(jnp.float32)).astype(jnp.bfloat16)
    wide = KVH * HD
    return total[:, :wide], total[:, wide:], full[:each], full[each:]


def solution(mesh):
    devices = mesh.devices.reshape(8, 4, 8, 2)
    mesh = Mesh(devices, ("y", "x", "z", "core"))
    rows, dp, seq = P(("y", "x", "z", "core"), None), P(DP, None), P(SEQ, None)
    return jax.shard_map(
        per_device,
        mesh=mesh,
        in_specs=(rows, rows, rows, rows, seq, seq, dp, dp, P()),
        out_specs=(rows, rows, seq, seq),
        check_vma=False,
    )
```

```python
import functools
import math

import jax
import jax.numpy as jnp
from jax import lax
from jax.experimental import pallas as pl
from jax.experimental.pallas import tpu as pltpu
from jax.sharding import Mesh, PartitionSpec as P

HQ = 48
KVH = 4
HD = 128
PLEN = 64
NT = (((1,), (1,)), ((), ()))
NN = (((1,), (0,)), ((), ()))
SEQ = ("z", "core")
SCALE = 1.0 / math.sqrt(HD)
TO_LOG2 = SCALE * math.log2(math.e)
F32 = jnp.float32
BF16 = jnp.bfloat16


def stacked(ref):
    return jnp.concatenate(
        [ref[:, j * HD : (j + 1) * HD] for j in range(ref.shape[1] // HD)], axis=0
    )


def joined(ref):
    return jnp.concatenate([ref[0, j : j + 1, :] for j in range(ref.shape[1])], axis=1)


def split(ref, row):
    for j in range(ref.shape[1]):
        ref[0, j : j + 1, :] = row[:, j * HD : (j + 1) * HD]


def token_stats_kernel(q_ref, g_ref, *refs):
    kv_refs, (bias_ref, top_ref, sum_ref, dot_ref) = refs[:-4], refs[-4:]
    blocks = len(kv_refs) // 2
    keys = jnp.concatenate([r[0] for r in kv_refs[:blocks]], axis=0)
    values = jnp.concatenate([r[0] for r in kv_refs[blocks:]], axis=0)
    toks = q_ref.shape[0]
    s_all = lax.dot_general(keys, stacked(q_ref), NT, preferred_element_type=F32)
    dp_all = lax.dot_general(values, stacked(g_ref), NT, preferred_element_type=F32)
    for j in range(q_ref.shape[1] // HD):
        cols = slice(j * toks, (j + 1) * toks)
        top = total = dot = None
        for b in range(blocks):
            rows = slice(b * toks, (b + 1) * toks)
            s = (s_all[rows, cols] + bias_ref[rows, :]).reshape(toks // 8, 8, toks)
            dp = dp_all[rows, cols].reshape(toks // 8, 8, toks)
            new = jnp.max(s, axis=0)
            new = new if top is None else jnp.maximum(top, new)
            e = jnp.exp2(s * TO_LOG2 - (new * TO_LOG2)[None])
            e_sum, e_dot = jnp.sum(e, axis=0), jnp.sum(e * dp, axis=0)
            if top is not None:
                old = jnp.exp2(top * TO_LOG2 - new * TO_LOG2)
                e_sum, e_dot = old * total + e_sum, old * dot + e_dot
            top, total, dot = new, e_sum, e_dot
        most = jnp.max(top, axis=0, keepdims=True)
        weight = jnp.exp2((top - most) * TO_LOG2)
        top_ref[0, j : j + 1, :] = most * TO_LOG2
        sum_ref[0, j : j + 1, :] = jnp.sum(total * weight, axis=0, keepdims=True)
        dot_ref[0, j : j + 1, :] = jnp.sum(dot * weight, axis=0, keepdims=True)


def prefix_kernel(
    core_ref, q_ref, g_ref, own_ref, other_ref, slot_ref, top_ref, sum_ref, dot_ref,
    lse_ref, delta_ref, mine_ref, theirs_ref,
):
    even = core_ref[0] == 0
    parts, _, each, _ = own_ref.shape

    def gathered(which):
        rows = []
        for part in range(parts):
            own, other = own_ref[part, which].astype(F32), other_ref[part, which].astype(F32)
            rows += [jnp.where(even, own, other), jnp.where(even, other, own)]
        return jnp.concatenate(rows, axis=0).astype(BF16)

    heads = q_ref.shape[1] // HD
    slot = jnp.concatenate([slot_ref[...]] * heads, axis=1)
    q, g = stacked(q_ref), stacked(g_ref)
    s_all = lax.dot_general(gathered(0), q, NT, preferred_element_type=F32)
    dp_all = lax.dot_general(gathered(1), g, NT, preferred_element_type=F32)
    slots = s_all.shape[0] // PLEN
    s, dp = s_all[:PLEN], dp_all[:PLEN]
    for k in range(1, slots):
        rows = slice(k * PLEN, (k + 1) * PLEN)
        s = jnp.where(slot == k, s_all[rows], s)
        dp = jnp.where(slot == k, dp_all[rows], dp)
    top = joined(top_ref)
    new = jnp.maximum(top, jnp.max(s, axis=0, keepdims=True) * TO_LOG2)
    e = jnp.exp2(s * TO_LOG2 - new)
    old = jnp.exp2(top - new)
    total = old * joined(sum_ref) + jnp.sum(e, axis=0, keepdims=True)
    dot = old * joined(dot_ref) + jnp.sum(e * dp, axis=0, keepdims=True)
    inverse = 1.0 / total
    delta = dot * inverse
    p = e * inverse
    ds = p * (dp - delta)
    split(lse_ref, new + jnp.log2(total))
    split(delta_ref, delta)
    zero = jnp.zeros_like(p)

    def spread(x):
        return jnp.concatenate(
            [jnp.where(slot == k, x, zero).astype(BF16) for k in range(slots)], axis=0
        )

    dk = lax.dot_general(spread(ds), q, NN, preferred_element_type=F32) * SCALE
    dv = lax.dot_general(spread(p), g, NN, preferred_element_type=F32)
    for which, grad in enumerate((dk, dv)):
        for part in range(parts):
            at = 2 * part * each
            low, high = grad[at : at + each], grad[at + each : at + 2 * each]
            mine_ref[part, which] = jnp.where(even, low, high)
            theirs_ref[part, which] = jnp.where(even, high, low)


def token_grads_kernel(q_ref, g_ref, *refs):
    kv_refs, (bias_ref, lse_ref, delta_ref, near_ref, far_ref) = refs[:-5], refs[-5:]
    blocks = len(kv_refs) // 2
    keys = jnp.concatenate([r[0] for r in kv_refs[:blocks]], axis=0)
    values = jnp.concatenate([r[0] for r in kv_refs[blocks:]], axis=0)
    heads = q_ref.shape[1] // HD
    q, g = stacked(q_ref), stacked(g_ref)
    bias = jnp.concatenate([bias_ref[...]] * heads, axis=1)
    s = lax.dot_general(keys, q, NT, preferred_element_type=F32) + bias
    dp = lax.dot_general(values, g, NT, preferred_element_type=F32)
    p = jnp.exp2(s * TO_LOG2 - joined(lse_ref))
    ds = (p * (dp - joined(delta_ref))).astype(BF16)
    dk = lax.dot_general(ds, q, NN, preferred_element_type=F32) * SCALE
    dv = lax.dot_general(p.astype(BF16), g, NN, preferred_element_type=F32)
    near = near_ref.shape[1]
    for which, grad in enumerate((dk, dv)):
        near_ref[which] = grad[:near]
        far_ref[which] = grad[near:].astype(BF16)


def plane(rows, which):
    return pl.BlockSpec((1, rows, HD), lambda h: (which, 0, h))


def planes(shape):
    lead = (0,) * (len(shape) - 1)
    return pl.BlockSpec((*shape[:-1], HD), lambda h: (*lead, h))


def whole(shape):
    return pl.BlockSpec(shape, lambda h: (0,) * len(shape))


def common(q):
    toks, width = q.shape
    run = width // KVH
    rows = pl.BlockSpec((toks, run), lambda h: (0, h))
    stat = pl.BlockSpec((1, run // HD, toks), lambda h: (h, 0, 0))
    return rows, stat, jax.ShapeDtypeStruct((KVH, run // HD, toks), F32)


def params(flops, exps):
    return dict(
        grid=(KVH,),
        compiler_params=pltpu.CompilerParams(vmem_limit_bytes=56 << 20),
        cost_estimate=pl.CostEstimate(flops=flops, bytes_accessed=5 << 20, transcendentals=exps),
    )


def token_stats(q, g, blocks, bias):
    rows, stat, shape = common(q)
    toks = q.shape[0]
    work = q.size // HD * bias.shape[0]
    return pl.pallas_call(
        token_stats_kernel,
        in_specs=[rows, rows]
        + [plane(toks, 0)] * len(blocks)
        + [plane(toks, 1)] * len(blocks)
        + [whole(bias.shape)],
        out_specs=[stat] * 3,
        out_shape=[shape] * 3,
        **params(4 * HD * work, work),
    )(q, g, *blocks, *blocks, bias)


def prefix_grads(core, q, g, own, other, slot, stats):
    rows, stat, shape = common(q)
    work = q.size // HD * 2 * own.shape[0] * own.shape[2]
    half = jax.ShapeDtypeStruct(own.shape, F32)
    return pl.pallas_call(
        prefix_kernel,
        in_specs=[pl.BlockSpec(memory_space=pltpu.SMEM), rows, rows]
        + [planes(own.shape)] * 2
        + [whole(slot.shape)]
        + [stat] * 3,
        out_specs=[stat, stat, planes(own.shape), planes(own.shape)],
        out_shape=[shape, shape, half, half],
        **params(8 * HD * work, work // 4),
    )(core, q, g, own, other, slot, *stats)


def token_grads(q, g, blocks, bias, lse, delta):
    rows, stat, _ = common(q)
    toks = q.shape[0]
    work = q.size // HD * bias.shape[0]
    near, far = (2, 3 * toks, KVH * HD), (2, 2 * toks, KVH * HD)
    return pl.pallas_call(
        token_grads_kernel,
        in_specs=[rows, rows]
        + [plane(toks, 0)] * len(blocks)
        + [plane(toks, 1)] * len(blocks)
        + [whole(bias.shape), stat, stat],
        out_specs=[planes(near), planes(far)],
        out_shape=[jax.ShapeDtypeStruct(near, F32), jax.ShapeDtypeStruct(far, BF16)],
        **params(8 * HD * work, work),
    )(q, g, *blocks, *blocks, bias, lse, delta)


def layout(lengths, tenants, slots, index, shards, toks):
    ends = jnp.cumsum(lengths)
    slot_of = jnp.sum(
        jnp.where(tenants[:, None] == jnp.arange(slots.shape[0])[None, :], slots[None, :], 0), axis=1
    )
    here = index * toks + jnp.arange(toks, dtype=jnp.int32)
    doc = jnp.sum((here[None, :] >= ends[:, None]).astype(jnp.int32), axis=0)
    pick = doc[None, :] == jnp.arange(lengths.shape[0])[:, None]
    first = jnp.sum(jnp.where(pick, (ends - lengths)[:, None], 0), axis=0)
    slot = jnp.sum(jnp.where(pick, slot_of[:, None], 0), axis=0)
    key = jnp.concatenate([s * toks + jnp.arange(toks, dtype=jnp.int32) for s in shards])
    ok = (key[:, None] >= first[None, :]) & (key[:, None] <= here[None, :])
    return jnp.where(ok, 0.0, -1e30).astype(F32), slot[None, :].astype(jnp.int32)


def per_device(
    queries, keys, values, grad_out, prefix_keys, prefix_values, doc_lengths, doc_tenants, tenant_slots
):
    toks = queries.shape[0]
    parts = lax.axis_size("z")
    count = parts * lax.axis_size("core")
    index, core = lax.axis_index(SEQ), lax.axis_index("core")
    even = core == 0

    def shift(x, steps):
        pairs = [(i, i + 2 * steps) for i in range(count) if 0 <= i + 2 * steps < count]
        return lax.ppermute(x, SEQ, pairs)

    def swap(x):
        return lax.ppermute(x, SEQ, [(i, i ^ 1) for i in range(count)])

    def exchange(x, axis):
        return lax.all_to_all(x, axis, split_axis=0, concat_axis=0, tiled=True)

    def to_all(x, axis):
        return exchange(jnp.broadcast_to(x[None], (lax.axis_size(axis), *x.shape)), axis)

    own = jnp.stack([keys, values])
    back1, back2 = shift(own, 1), shift(own, 2)
    pref_own = to_all(jnp.stack([prefix_keys, prefix_values]), "z")
    cross1 = swap(back1)
    cross02 = swap(jnp.where(even, own, back2))
    shards = [
        index - 4,
        index - 2,
        index,
        jnp.where(even, index - 3, index - 1),
        jnp.where(even, index - 1, index - 3),
    ]
    blocks = (back2, back1, own, cross02, cross1)
    bias, slot = layout(doc_lengths[0], doc_tenants[0], tenant_slots, index, shards, toks)
    stats = token_stats(queries, grad_out, blocks, bias)
    pref_other = swap(pref_own)
    lse, delta, mine, theirs = prefix_grads(
        core.astype(jnp.int32)[None], queries, grad_out, pref_own, pref_other, slot, stats
    )

    mine = (mine + swap(theirs)).astype(BF16)
    rows = jnp.sum(exchange(mine, "z").astype(F32), axis=0)
    rows = jnp.sum(to_all(rows, "x"), axis=0)
    rows = jnp.sum(to_all(rows.astype(BF16), "y").astype(F32), axis=0)

    near, far = token_grads(queries, grad_out, blocks, bias, lse, delta)
    far = swap(far).astype(F32)
    zero = jnp.zeros((2, toks, far.shape[2]), F32)
    two = near[:, :toks] + jnp.where(even, zero, far[:, :toks])
    one = near[:, toks : 2 * toks] + far[:, toks:]
    home = near[:, 2 * toks :] + jnp.where(even, far[:, :toks], zero)
    one = shift(one.astype(BF16), -1)
    two = shift(two.astype(BF16), -2)
    total = (home + one.astype(F32) + two.astype(F32)).astype(BF16)
    return total[0], total[1], rows[0], rows[1]


def solution(mesh):
    mesh = Mesh(mesh.devices.reshape(8, 4, 8, 2), ("y", "x", "z", "core"))
    rows, dp, seq = P(("y", "x", "z", "core"), None), P(("y", "x"), None), P(SEQ, None)
    return jax.shard_map(
        per_device,
        mesh=mesh,
        in_specs=(rows, rows, rows, rows, seq, seq, dp, dp, P()),
        out_specs=(rows, rows, seq, seq),
        check_vma=False,
    )
```

```python
import functools
import math

import jax
import jax.numpy as jnp
from jax import lax
from jax.experimental import pallas as pl
from jax.experimental.pallas import tpu as pltpu
from jax.sharding import Mesh, PartitionSpec as P

HQ = 48
KVH = 4
HD = 128
PLEN = 64
NT = (((1,), (1,)), ((), ()))
NN = (((1,), (0,)), ((), ()))
SEQ = ("z", "core")
SCALE = 1.0 / math.sqrt(HD)
TO_LOG2 = SCALE * math.log2(math.e)
F32 = jnp.float32
BF16 = jnp.bfloat16


def stacked(ref, lead=()):
    count = ref.shape[-1] // HD
    return jnp.concatenate(
        [ref[(*lead, slice(None), slice(j * HD, (j + 1) * HD))] for j in range(count)], axis=0
    )


def joined(ref, chunk):
    return jnp.concatenate([ref[0, chunk, j : j + 1, :] for j in range(ref.shape[2])], axis=1)


def split(ref, chunk, row):
    for j in range(ref.shape[2]):
        ref[0, chunk, j : j + 1, :] = row[:, j * HD : (j + 1) * HD]


def windows(even, own, one, two, cross):
    last = jnp.where(even, own[0].astype(F32), two[0].astype(F32)).astype(BF16)
    far = jnp.where(even, cross[2, 0].astype(F32), cross[0, 0].astype(F32)).astype(BF16)
    return (
        jnp.concatenate([own[0], one[0], two[0], cross[1, 0], far], axis=0),
        jnp.concatenate([cross[0, 0], one[0], cross[1, 0], cross[2, 0], last], axis=0),
    )


def token_stats_kernel(core_ref, q_ref, g_ref, qo_ref, go_ref, *refs):
    bias_ref, top_ref, sum_ref, dot_ref = refs[8:]
    even = core_ref[0] == 0
    keys, values = windows(even, *refs[:4]), windows(even, *refs[4:8])
    toks = q_ref.shape[0]
    blocks = keys[0].shape[0] // toks
    for chunk in range(2):
        q, g = (stacked(qo_ref, (0,)), stacked(go_ref, (0,))) if chunk else (stacked(q_ref), stacked(g_ref))
        s_all = lax.dot_general(keys[chunk], q, NT, preferred_element_type=F32)
        dp_all = lax.dot_general(values[chunk], g, NT, preferred_element_type=F32)
        for j in range(q_ref.shape[1] // HD):
            cols = slice(j * toks, (j + 1) * toks)
            top = total = dot = None
            for b in range(blocks):
                rows = slice(b * toks, (b + 1) * toks)
                s = (s_all[rows, cols] + bias_ref[chunk, rows, :]).reshape(toks // 8, 8, toks)
                dp = dp_all[rows, cols].reshape(toks // 8, 8, toks)
                new = jnp.max(s, axis=0)
                new = new if top is None else jnp.maximum(top, new)
                e = jnp.exp2(s * TO_LOG2 - (new * TO_LOG2)[None])
                e_sum, e_dot = jnp.sum(e, axis=0), jnp.sum(e * dp, axis=0)
                if top is not None:
                    old = jnp.exp2(top * TO_LOG2 - new * TO_LOG2)
                    e_sum, e_dot = old * total + e_sum, old * dot + e_dot
                top, total, dot = new, e_sum, e_dot
            most = jnp.max(top, axis=0, keepdims=True)
            weight = jnp.exp2((top - most) * TO_LOG2)
            top_ref[0, chunk, j : j + 1, :] = most * TO_LOG2
            sum_ref[0, chunk, j : j + 1, :] = jnp.sum(total * weight, axis=0, keepdims=True)
            dot_ref[0, chunk, j : j + 1, :] = jnp.sum(dot * weight, axis=0, keepdims=True)


def prefix_kernel(
    core_ref, q_ref, g_ref, qo_ref, go_ref, pref_ref, slot_ref, top_ref, sum_ref, dot_ref,
    lse_ref, delta_ref, out_ref,
):
    count, _, each, _ = pref_ref.shape

    def gathered(which):
        rows = [pref_ref[part, which].astype(F32) for part in range(count)]
        return jnp.concatenate(rows, axis=0).astype(BF16)

    keys, values = gathered(0), gathered(1)
    heads = q_ref.shape[1] // HD
    slots = keys.shape[0] // PLEN
    grads = []
    for chunk in range(2):
        q, g = (stacked(qo_ref, (0,)), stacked(go_ref, (0,))) if chunk else (stacked(q_ref), stacked(g_ref))
        slot = jnp.concatenate([slot_ref[chunk]] * heads, axis=1)
        s_all = lax.dot_general(keys, q, NT, preferred_element_type=F32)
        dp_all = lax.dot_general(values, g, NT, preferred_element_type=F32)
        s, dp = s_all[:PLEN], dp_all[:PLEN]
        for k in range(1, slots):
            rows = slice(k * PLEN, (k + 1) * PLEN)
            s = jnp.where(slot == k, s_all[rows], s)
            dp = jnp.where(slot == k, dp_all[rows], dp)
        top = joined(top_ref, chunk)
        new = jnp.maximum(top, jnp.max(s, axis=0, keepdims=True) * TO_LOG2)
        e = jnp.exp2(s * TO_LOG2 - new)
        old = jnp.exp2(top - new)
        total = old * joined(sum_ref, chunk) + jnp.sum(e, axis=0, keepdims=True)
        dot = old * joined(dot_ref, chunk) + jnp.sum(e * dp, axis=0, keepdims=True)
        inverse = 1.0 / total
        delta = dot * inverse
        p = e * inverse
        ds = p * (dp - delta)
        split(lse_ref, chunk, new + jnp.log2(total))
        split(delta_ref, chunk, delta)
        zero = jnp.zeros_like(p)

        def spread(x, slot=slot, zero=zero):
            return jnp.concatenate(
                [jnp.where(slot == k, x, zero).astype(BF16) for k in range(slots)], axis=0
            )

        grads.append(
            (
                lax.dot_general(spread(ds), q, NN, preferred_element_type=F32),
                lax.dot_general(spread(p), g, NN, preferred_element_type=F32),
            )
        )
    dk, dv = (grads[0][0] + grads[1][0]) * SCALE, grads[0][1] + grads[1][1]
    for which, grad in enumerate((dk, dv)):
        for part in range(count):
            out_ref[part, which] = grad[part * each : (part + 1) * each].astype(BF16)


def token_grads_kernel(core_ref, q_ref, g_ref, qo_ref, go_ref, *refs):
    bias_ref, lse_ref, delta_ref, home_ref, one_ref, two_ref = refs[8:]
    even = core_ref[0] == 0
    keys, values = windows(even, *refs[:4]), windows(even, *refs[4:8])
    toks = q_ref.shape[0]
    heads = q_ref.shape[1] // HD
    found = []
    for chunk in range(2):
        q, g = (stacked(qo_ref, (0,)), stacked(go_ref, (0,))) if chunk else (stacked(q_ref), stacked(g_ref))
        bias = jnp.concatenate([bias_ref[chunk]] * heads, axis=1)
        s = lax.dot_general(keys[chunk], q, NT, preferred_element_type=F32) + bias
        dp = lax.dot_general(values[chunk], g, NT, preferred_element_type=F32)
        p = jnp.exp2(s * TO_LOG2 - joined(lse_ref, chunk))
        ds = (p * (dp - joined(delta_ref, chunk))).astype(BF16)
        dk = lax.dot_general(ds, q, NN, preferred_element_type=F32) * SCALE
        dv = lax.dot_general(p.astype(BF16), g, NN, preferred_element_type=F32)
        found.append((dk, dv))
    for which in range(2):
        a, b = (
            [found[chunk][which][n * toks : (n + 1) * toks] for n in range(5)] for chunk in range(2)
        )
        zero = jnp.zeros_like(a[4])
        home_ref[which, :toks] = a[0] + jnp.where(even, b[4], zero)
        home_ref[which, toks:] = b[0] + jnp.where(even, zero, a[4])
        one_ref[which, :toks] = (a[1] + b[1]).astype(BF16)
        one_ref[which, toks:] = (a[3] + b[2]).astype(BF16)
        two_ref[which, :toks] = (a[2] + jnp.where(even, zero, b[4])).astype(BF16)
        two_ref[which, toks:] = (b[3] + jnp.where(even, a[4], zero)).astype(BF16)


def planes(shape):
    lead = (0,) * (len(shape) - 1)
    return pl.BlockSpec((*shape[:-1], HD), lambda h, core: (*lead, h))


def whole(shape):
    return pl.BlockSpec(shape, lambda h, core: (0,) * len(shape))


def call(kernel, core, queries, others, flops, exps, ins, outs):
    q, g = queries
    toks, run, kept = q.shape[0], q.shape[1] // KVH, KVH // 2
    mine = pl.BlockSpec((toks, run), lambda h, core: (0, core[0] * kept + h))
    theirs = [
        pl.BlockSpec((1, toks, run), lambda h, core, which=which: (which, 0, h)) for which in range(2)
    ]
    return pl.pallas_call(
        kernel,
        grid_spec=pltpu.PrefetchScalarGridSpec(
            num_scalar_prefetch=1,
            grid=(kept,),
            in_specs=[mine, mine, *theirs] + [block for _, block in ins],
            out_specs=[block for _, block in outs],
        ),
        out_shape=[shape for shape, _ in outs],
        compiler_params=pltpu.CompilerParams(vmem_limit_bytes=56 << 20),
        cost_estimate=pl.CostEstimate(flops=flops, bytes_accessed=5 << 20, transcendentals=exps),
    )(core, q, g, others, others, *[array for array, _ in ins])


def stat(q):
    shape = (KVH // 2, 2, HQ // KVH, q.shape[0])
    block = pl.BlockSpec((1, *shape[1:]), lambda h, core: (h, 0, 0, 0))
    return jax.ShapeDtypeStruct(shape, F32), block


def window_ins(own, one, two, cross, bias):
    toks, kept = own.shape[1], KVH // 2
    ins = []
    for which in range(2):
        at = pl.BlockSpec((1, toks, HD), lambda h, core, which=which: (which, 0, core[0] * kept + h))
        far = pl.BlockSpec((3, 1, toks, HD), lambda h, core, which=which: (0, which, 0, h))
        ins += [(own, at), (one, at), (two, at), (cross, far)]
    return ins + [(bias, whole(bias.shape))]


def layout(lengths, tenants, slots, block, shards, toks):
    ends = jnp.cumsum(lengths)
    slot_of = jnp.sum(
        jnp.where(tenants[:, None] == jnp.arange(slots.shape[0])[None, :], slots[None, :], 0), axis=1
    )
    here = block * toks + jnp.arange(toks, dtype=jnp.int32)
    doc = jnp.sum((here[None, :] >= ends[:, None]).astype(jnp.int32), axis=0)
    pick = doc[None, :] == jnp.arange(lengths.shape[0])[:, None]
    first = jnp.sum(jnp.where(pick, (ends - lengths)[:, None], 0), axis=0)
    slot = jnp.sum(jnp.where(pick, slot_of[:, None], 0), axis=0)
    key = jnp.concatenate([s * toks + jnp.arange(toks, dtype=jnp.int32) for s in shards])
    ok = (key[:, None] >= first[None, :]) & (key[:, None] <= here[None, :])
    return jnp.where(ok, 0.0, -1e30).astype(F32), slot[None, :].astype(jnp.int32)


def per_device(
    queries, keys, values, grad_out, prefix_keys, prefix_values, doc_lengths, doc_tenants, tenant_slots
):
    toks, width = queries.shape
    parts = lax.axis_size("z")
    count = parts * 2
    index, core = lax.axis_index(SEQ), lax.axis_index("core").astype(jnp.int32)
    even = core == 0
    cores = core[None]

    def shift(x, steps):
        pairs = [(i, i + 2 * steps) for i in range(count) if 0 <= i + 2 * steps < count]
        return lax.ppermute(x, SEQ, pairs)

    def swap(x):
        return lax.ppermute(x, SEQ, [(i, i ^ 1) for i in range(count)])

    def exchange(x, axis):
        return lax.all_to_all(x, axis, split_axis=0, concat_axis=0, tiled=True)

    def to_all(x, axis):
        return exchange(jnp.broadcast_to(x[None], (lax.axis_size(axis), *x.shape)), axis)

    def other_half(x):
        half = x.shape[-1] // 2
        return jnp.where(even, x[..., half:], x[..., :half])

    own = jnp.stack([keys, values])
    one, two = shift(own, 1), shift(own, 2)
    pref = jnp.stack([prefix_keys, prefix_values])
    pref = pref.reshape(2, -1, 2, KVH * HD // 2).transpose(2, 0, 1, 3)
    pref = jnp.broadcast_to(pref[None], (parts, *pref.shape)).reshape(count, *pref.shape[1:])
    pref = exchange(pref, SEQ)
    others = swap(jnp.stack([other_half(queries), other_half(grad_out)]))
    cross = swap(jnp.stack([other_half(own), other_half(one), other_half(two)]))

    facing = index ^ 1
    near, far = jnp.where(even, index - 1, index - 3), jnp.where(even, index - 3, index - 1)
    docs = (doc_lengths[0], doc_tenants[0], tenant_slots)
    shards = [index, index - 2, index - 4, near, far]
    bias0, slot0 = layout(*docs, index, shards, toks)
    last = jnp.where(even, index, index - 4)
    shards = [facing, index - 2, facing - 2, facing - 4, last]
    bias1, slot1 = layout(*docs, facing, shards, toks)
    bias, slot = jnp.stack([bias0, bias1]), jnp.stack([slot0, slot1])

    run = functools.partial(call, core=cores, queries=(queries, grad_out), others=others)
    stats = stat(queries)
    work = queries.size // HD * bias.shape[1]
    window = window_ins(own, one, two, cross, bias)
    top, total, dot = run(
        token_stats_kernel, flops=4 * HD * work, exps=work, ins=window, outs=[stats] * 3
    )
    prefs = queries.size // HD * count * pref.shape[2]
    lse, delta, rows = run(
        prefix_kernel,
        flops=8 * HD * prefs,
        exps=prefs // 6,
        ins=[(pref, planes(pref.shape)), (slot, whole(slot.shape))]
        + [(x, stats[1]) for x in (top, total, dot)],
        outs=[stats, stats, (jax.ShapeDtypeStruct(pref.shape, BF16), planes(pref.shape))],
    )

    rows = exchange(rows, SEQ).astype(F32)
    rows = jnp.sum(rows.reshape(parts, 2, *rows.shape[1:]), axis=0)
    rows = jnp.sum(to_all(rows, "x"), axis=0)
    rows = jnp.sum(to_all(rows.astype(BF16), "y").astype(F32), axis=0)
    rows = rows.transpose(1, 2, 0, 3).reshape(2, prefix_keys.shape[0], KVH * HD)

    wide = (2, 2 * toks, KVH * HD // 2)
    home, back1, back2 = run(
        token_grads_kernel,
        flops=8 * HD * work,
        exps=work,
        ins=window + [(lse, stats[1]), (delta, stats[1])],
        outs=[
            (jax.ShapeDtypeStruct(wide, F32), planes(wide)),
            (jax.ShapeDtypeStruct(wide, BF16), planes(wide)),
            (jax.ShapeDtypeStruct(wide, BF16), planes(wide)),
        ],
    )
    back1, back2 = shift(back1, -1), shift(back2, -2)
    grads = (home + back1.astype(F32) + back2.astype(F32)).astype(BF16)
    mine, theirs = grads[:, :toks], swap(grads[:, toks:])
    grads = jnp.concatenate(
        [jnp.where(even, mine, theirs), jnp.where(even, theirs, mine)], axis=2
    )
    return grads[0], grads[1], rows[0], rows[1]


def solution(mesh):
    mesh = Mesh(mesh.devices.reshape(8, 4, 8, 2), ("y", "x", "z", "core"))
    rows, dp, seq = P(("y", "x", "z", "core"), None), P(("y", "x"), None), P(SEQ, None)
    return jax.shard_map(
        per_device,
        mesh=mesh,
        in_specs=(rows, rows, rows, rows, seq, seq, dp, dp, P()),
        out_specs=(rows, rows, seq, seq),
        check_vma=False,
    )
```

```python
import math

import jax
import jax.numpy as jnp
from jax import lax
from jax.experimental import pallas as pl
from jax.experimental.pallas import tpu as pltpu
from jax.sharding import Mesh, PartitionSpec as P

HQ = 48
KVH = 4
HD = 128
PLEN = 64
NT = (((1,), (1,)), ((), ()))
NN = (((1,), (0,)), ((), ()))
SEQ = ("z", "core")
SCALE = 1.0 / math.sqrt(HD)
TO_LOG2 = SCALE * math.log2(math.e)
F32 = jnp.float32
BF16 = jnp.bfloat16
VMEM_BYTES = 20 << 20


def heads_of(ref, start, count, lead=()):
    columns = [slice(start + j * HD, start + (j + 1) * HD) for j in range(count)]
    return jnp.concatenate([ref[(*lead, slice(None), c)] for c in columns], axis=0)


def joined(ref, kind, h, chunk):
    return jnp.concatenate([ref[kind, h, chunk, j : j + 1, :] for j in range(ref.shape[3])], axis=1)


def split(ref, kind, h, chunk, row):
    for j in range(ref.shape[3]):
        ref[kind, h, chunk, j : j + 1, :] = row[:, j * HD : (j + 1) * HD]


def units(mine_ref, others_ref):
    kept = KVH // 2
    run = mine_ref.shape[2] // kept
    found = []
    for h in range(kept):
        for chunk, ref in enumerate((mine_ref, others_ref)):

            def read(which, first, count, h=h, ref=ref):
                return heads_of(ref, h * run + first * HD, count, (which,))

            found.append((h, chunk, read))
    return found, run // HD


def windows(core, h, which, own_ref, one_ref, two_ref, cross_ref):
    at = pl.ds(pl.multiple_of((core * (KVH // 2) + h) * HD, HD), HD)
    own, one, two = (ref[which, :, at] for ref in (own_ref, one_ref, two_ref))
    cross = [cross_ref[n, which, :, h * HD : (h + 1) * HD] for n in range(3)]
    even = core == 0
    last = jnp.where(even, own.astype(F32), two.astype(F32)).astype(BF16)
    far = jnp.where(even, cross[2].astype(F32), cross[0].astype(F32)).astype(BF16)
    return (
        jnp.concatenate([own, one, two, cross[1], far], axis=0),
        jnp.concatenate([cross[0], one, cross[1], cross[2], last], axis=0),
    )


def token_stats_kernel(core_ref, mine_ref, others_ref, *refs):
    window, (bias_ref, stat_ref) = refs[:4], refs[4:]
    core = core_ref[0]
    toks = mine_ref.shape[1]
    blocks = bias_ref.shape[1] // toks
    found, heads = units(mine_ref, others_ref)
    for h, chunk, read in found:
        keys, values = (windows(core, h, which, *window)[chunk] for which in range(2))

        def dots(j, keys=keys, values=values, read=read):
            return (
                lax.dot_general(keys, read(0, j, 1), NT, preferred_element_type=F32),
                lax.dot_general(values, read(1, j, 1), NT, preferred_element_type=F32),
            )

        ahead = dots(0)
        for j in range(heads):
            s_all, dp_all = ahead
            if j + 1 < heads:
                ahead = dots(j + 1)
            top = total = dot = None
            for b in range(blocks):
                rows = slice(b * toks, (b + 1) * toks)
                s = (s_all[rows] + bias_ref[chunk, rows, :]).reshape(toks // 8, 8, toks)
                dp = dp_all[rows].reshape(toks // 8, 8, toks)
                new = jnp.max(s, axis=0)
                new = new if top is None else jnp.maximum(top, new)
                e = jnp.exp2(s * TO_LOG2 - (new * TO_LOG2)[None])
                e_sum, e_dot = jnp.sum(e, axis=0), jnp.sum(e * dp, axis=0)
                if top is not None:
                    old = jnp.exp2(top * TO_LOG2 - new * TO_LOG2)
                    e_sum, e_dot = old * total + e_sum, old * dot + e_dot
                top, total, dot = new, e_sum, e_dot
            most = jnp.max(top, axis=0, keepdims=True)
            weight = jnp.exp2((top - most) * TO_LOG2)
            stat_ref[0, h, chunk, j : j + 1, :] = most * TO_LOG2
            stat_ref[1, h, chunk, j : j + 1, :] = jnp.sum(total * weight, axis=0, keepdims=True)
            stat_ref[2, h, chunk, j : j + 1, :] = jnp.sum(dot * weight, axis=0, keepdims=True)


def prefix_kernel(mine_ref, others_ref, pref_ref, slot_ref, stat_ref, full_ref, out_ref):
    count, _, each, _ = pref_ref.shape
    found, heads = units(mine_ref, others_ref)
    slots = count * each // PLEN
    grads = {}
    for h, chunk, read in found:
        columns = slice(h * HD, (h + 1) * HD)
        keys, values = (
            jnp.concatenate(
                [pref_ref[part, which, :, columns].astype(F32) for part in range(count)], axis=0
            ).astype(BF16)
            for which in range(2)
        )
        q, g = read(0, 0, heads), read(1, 0, heads)
        slot = jnp.concatenate([slot_ref[chunk]] * heads, axis=1)
        s_all = lax.dot_general(keys, q, NT, preferred_element_type=F32)
        dp_all = lax.dot_general(values, g, NT, preferred_element_type=F32)
        s, dp = s_all[:PLEN], dp_all[:PLEN]
        for k in range(1, slots):
            rows = slice(k * PLEN, (k + 1) * PLEN)
            s = jnp.where(slot == k, s_all[rows], s)
            dp = jnp.where(slot == k, dp_all[rows], dp)
        top = joined(stat_ref, 0, h, chunk)
        new = jnp.maximum(top, jnp.max(s, axis=0, keepdims=True) * TO_LOG2)
        e = jnp.exp2(s * TO_LOG2 - new)
        old = jnp.exp2(top - new)
        total = old * joined(stat_ref, 1, h, chunk) + jnp.sum(e, axis=0, keepdims=True)
        dot = old * joined(stat_ref, 2, h, chunk) + jnp.sum(e * dp, axis=0, keepdims=True)
        inverse = 1.0 / total
        delta = dot * inverse
        p = e * inverse
        ds = p * (dp - delta)
        split(full_ref, 0, h, chunk, new + jnp.log2(total))
        split(full_ref, 1, h, chunk, delta)
        zero = jnp.zeros_like(p)

        def spread(x, slot=slot, zero=zero):
            return jnp.concatenate(
                [jnp.where(slot == k, x, zero).astype(BF16) for k in range(slots)], axis=0
            )

        grads[chunk] = (
            lax.dot_general(spread(ds), q, NN, preferred_element_type=F32),
            lax.dot_general(spread(p), g, NN, preferred_element_type=F32),
        )
        if chunk:
            dk, dv = (grads[0][0] + grads[1][0]) * SCALE, grads[0][1] + grads[1][1]
            for which, grad in enumerate((dk, dv)):
                for part in range(count):
                    rows = grad[part * each : (part + 1) * each]
                    out_ref[part, which, :, columns] = rows.astype(BF16)


def token_grads_kernel(core_ref, mine_ref, others_ref, *refs):
    window, (bias_ref, full_ref, home_ref, one_ref, two_ref) = refs[:4], refs[4:]
    core = core_ref[0]
    even = core == 0
    toks = mine_ref.shape[1]
    found, heads = units(mine_ref, others_ref)
    grads = {}
    for h, chunk, read in found:
        keys, values = (windows(core, h, which, *window)[chunk] for which in range(2))
        q, g = read(0, 0, heads), read(1, 0, heads)
        bias = jnp.concatenate([bias_ref[chunk]] * heads, axis=1)
        s = lax.dot_general(keys, q, NT, preferred_element_type=F32) + bias
        dp = lax.dot_general(values, g, NT, preferred_element_type=F32)
        p = jnp.exp2(s * TO_LOG2 - joined(full_ref, 0, h, chunk))
        ds = (p * (dp - joined(full_ref, 1, h, chunk))).astype(BF16)
        dk = lax.dot_general(ds, q, NN, preferred_element_type=F32) * SCALE
        dv = lax.dot_general(p.astype(BF16), g, NN, preferred_element_type=F32)
        grads[chunk] = (dk, dv)
        if not chunk:
            continue
        columns = slice(h * HD, (h + 1) * HD)
        for which in range(2):
            a, b = (
                [grads[c][which][n * toks : (n + 1) * toks] for n in range(5)] for c in range(2)
            )
            zero = jnp.zeros_like(a[4])
            home_ref[which, :toks, columns] = a[0] + jnp.where(even, b[4], zero)
            home_ref[which, toks:, columns] = b[0] + jnp.where(even, zero, a[4])
            one_ref[which, :toks, columns] = (a[1] + b[1]).astype(BF16)
            one_ref[which, toks:, columns] = (a[3] + b[2]).astype(BF16)
            two_ref[which, :toks, columns] = (a[2] + jnp.where(even, zero, b[4])).astype(BF16)
            two_ref[which, toks:, columns] = (b[3] + jnp.where(even, a[4], zero)).astype(BF16)


def call(kernel, flops, exps, ins, outs):
    space = pl.BlockSpec(memory_space=pltpu.VMEM)
    scalar = pl.BlockSpec(memory_space=pltpu.SMEM)
    return pl.pallas_call(
        kernel,
        in_specs=[scalar if x.ndim == 1 else space for x in ins],
        out_specs=[space] * len(outs),
        out_shape=outs,
        compiler_params=pltpu.CompilerParams(vmem_limit_bytes=VMEM_BYTES),
        cost_estimate=pl.CostEstimate(flops=flops, bytes_accessed=6 << 20, transcendentals=exps),
    )(*ins)


def layout(lengths, tenants, slots, block, shards, toks):
    ends = jnp.cumsum(lengths)
    slot_of = jnp.sum(
        jnp.where(tenants[:, None] == jnp.arange(slots.shape[0])[None, :], slots[None, :], 0), axis=1
    )
    here = block * toks + jnp.arange(toks, dtype=jnp.int32)
    doc = jnp.sum((here[None, :] >= ends[:, None]).astype(jnp.int32), axis=0)
    pick = doc[None, :] == jnp.arange(lengths.shape[0])[:, None]
    first = jnp.sum(jnp.where(pick, (ends - lengths)[:, None], 0), axis=0)
    slot = jnp.sum(jnp.where(pick, slot_of[:, None], 0), axis=0)
    key = jnp.concatenate([s * toks + jnp.arange(toks, dtype=jnp.int32) for s in shards])
    ok = (key[:, None] >= first[None, :]) & (key[:, None] <= here[None, :])
    return jnp.where(ok, 0.0, -1e30).astype(F32), slot[None, :].astype(jnp.int32)


def per_device(
    queries, keys, values, grad_out, prefix_keys, prefix_values, doc_lengths, doc_tenants, tenant_slots
):
    toks, width = queries.shape
    parts = lax.axis_size("z")
    count = parts * 2
    index, core = lax.axis_index(SEQ), lax.axis_index("core").astype(jnp.int32)
    even = core == 0
    cores = core[None]

    def shift(x, steps):
        pairs = [(i, i + 2 * steps) for i in range(count) if 0 <= i + 2 * steps < count]
        return lax.ppermute(x, SEQ, pairs)

    def swap(x):
        return lax.ppermute(x, SEQ, [(i, i ^ 1) for i in range(count)])

    def exchange(x, axis):
        return lax.all_to_all(x, axis, split_axis=0, concat_axis=0, tiled=True)

    def to_all(x, axis):
        return exchange(jnp.broadcast_to(x[None], (lax.axis_size(axis), *x.shape)), axis)

    def half(x, which):
        size = x.shape[-1] // 2
        return lax.dynamic_slice_in_dim(x, which * size, size, x.ndim - 1)

    def other_half(x):
        return half(x, 1 - core)

    own = jnp.stack([keys, values])
    one, two = shift(own, 1), shift(own, 2)
    pref = jnp.stack([prefix_keys, prefix_values])
    pref = pref.reshape(2, -1, 2, KVH * HD // 2).transpose(2, 0, 1, 3)
    pref = jnp.broadcast_to(pref[None], (parts, *pref.shape)).reshape(count, *pref.shape[1:])
    pref = exchange(pref, SEQ)
    others = swap(jnp.stack([other_half(queries), other_half(grad_out)]))
    cross = swap(jnp.stack([other_half(own), other_half(one), other_half(two)]))

    facing = index ^ 1
    near, far = jnp.where(even, index - 1, index - 3), jnp.where(even, index - 3, index - 1)
    docs = (doc_lengths[0], doc_tenants[0], tenant_slots)
    shards = [index, index - 2, index - 4, near, far]
    bias0, slot0 = layout(*docs, index, shards, toks)
    last = jnp.where(even, index, index - 4)
    shards = [facing, index - 2, facing - 2, facing - 4, last]
    bias1, slot1 = layout(*docs, facing, shards, toks)
    bias, slot = jnp.stack([bias0, bias1]), jnp.stack([slot0, slot1])

    heads = [jnp.stack([half(queries, core), half(grad_out, core)]), others]
    shape = (KVH // 2, 2, HQ // KVH, toks)
    work = queries.size // HD * bias.shape[1]
    window = [cores, *heads, own, one, two, cross, bias]
    (stats,) = call(
        token_stats_kernel,
        flops=4 * HD * work,
        exps=work,
        ins=window,
        outs=[jax.ShapeDtypeStruct((3, *shape), F32)],
    )
    prefs = queries.size // HD * count * pref.shape[2]
    full, rows = call(
        prefix_kernel,
        flops=8 * HD * prefs,
        exps=prefs // 6,
        ins=[*heads, pref, slot, stats],
        outs=[jax.ShapeDtypeStruct((2, *shape), F32), jax.ShapeDtypeStruct(pref.shape, BF16)],
    )
    wide = (2, 2 * toks, KVH * HD // 2)
    home, back1, back2 = call(
        token_grads_kernel,
        flops=8 * HD * work,
        exps=work,
        ins=window + [full],
        outs=[jax.ShapeDtypeStruct(wide, kind) for kind in (F32, BF16, BF16)],
    )

    rows = exchange(rows, SEQ).astype(F32)
    rows = rows.reshape(parts, 2, *rows.shape[1:])
    rows = jnp.concatenate([jnp.sum(rows[:, n], axis=0) for n in range(2)], axis=2)
    rows, home, back1, back2 = lax.optimization_barrier((rows.astype(BF16), home, back1, back2))
    rows = jnp.sum(to_all(rows, "x").astype(F32), axis=0)
    rows = to_all(rows.astype(BF16), "y").astype(F32)

    back1, back2 = shift(back1, -1), shift(back2, -2)
    grads = (home + back1.astype(F32) + back2.astype(F32)).astype(BF16)
    mine, theirs = grads[:, :toks], swap(grads[:, toks:])
    grads = jnp.concatenate(
        [jnp.where(even, mine, theirs), jnp.where(even, theirs, mine)], axis=2
    )
    return grads[0], grads[1], jnp.sum(rows[:, 0], axis=0), jnp.sum(rows[:, 1], axis=0)


def solution(mesh):
    mesh = Mesh(mesh.devices.reshape(8, 4, 8, 2), ("y", "x", "z", "core"))
    rows, dp, seq = P(("y", "x", "z", "core"), None), P(("y", "x"), None), P(SEQ, None)
    return jax.shard_map(
        per_device,
        mesh=mesh,
        in_specs=(rows, rows, rows, rows, seq, seq, dp, dp, P()),
        out_specs=(rows, rows, seq, seq),
        check_vma=False,
    )
```

```python
import math

import jax
import jax.numpy as jnp
from jax import lax
from jax.experimental import pallas as pl
from jax.experimental.pallas import tpu as pltpu
from jax.sharding import Mesh, PartitionSpec as P

HQ = 48
KVH = 4
HD = 128
PLEN = 64
NT = (((1,), (1,)), ((), ()))
NN = (((1,), (0,)), ((), ()))
SEQ = ("z", "core")
DP = ("y", "x")
SCALE = 1.0 / math.sqrt(HD)
TO_LOG2 = SCALE * math.log2(math.e)
F32 = jnp.float32
BF16 = jnp.bfloat16
VMEM_BYTES = 20 << 20


def heads_of(ref, start, count, lead=()):
    columns = [slice(start + j * HD, start + (j + 1) * HD) for j in range(count)]
    return jnp.concatenate([ref[(*lead, slice(None), c)] for c in columns], axis=0)


def joined(ref, kind, h, chunk):
    return jnp.concatenate([ref[kind, h, chunk, j : j + 1, :] for j in range(ref.shape[3])], axis=1)


def split(ref, kind, h, chunk, row):
    for j in range(ref.shape[3]):
        ref[kind, h, chunk, j : j + 1, :] = row[:, j * HD : (j + 1) * HD]


def units(mine_ref, others_ref):
    kept = KVH // 2
    run = mine_ref.shape[2] // kept
    found = []
    for h in range(kept):
        for chunk, ref in enumerate((mine_ref, others_ref)):

            def read(which, first, count, h=h, ref=ref):
                return heads_of(ref, h * run + first * HD, count, (which,))

            found.append((h, chunk, read))
    return found, run // HD


def windows(core, h, which, own_ref, one_ref, two_ref, cross_ref):
    at = pl.ds(pl.multiple_of((core * (KVH // 2) + h) * HD, HD), HD)
    own, one, two = (ref[which, :, at] for ref in (own_ref, one_ref, two_ref))
    cross = [cross_ref[n, which, :, h * HD : (h + 1) * HD] for n in range(3)]
    even = core == 0
    last = jnp.where(even, own.astype(F32), two.astype(F32)).astype(BF16)
    far = jnp.where(even, cross[2].astype(F32), cross[0].astype(F32)).astype(BF16)
    return (
        jnp.concatenate([own, one, two, cross[1], far], axis=0),
        jnp.concatenate([cross[0], one, cross[1], cross[2], last], axis=0),
    )


def token_stats_kernel(core_ref, mine_ref, others_ref, *refs):
    window, (bias_ref, stat_ref) = refs[:4], refs[4:]
    core = core_ref[0]
    toks = mine_ref.shape[1]
    blocks = bias_ref.shape[1] // toks
    found, heads = units(mine_ref, others_ref)
    for h, chunk, read in found:
        keys, values = (windows(core, h, which, *window)[chunk] for which in range(2))

        def dots(j, keys=keys, values=values, read=read):
            return (
                lax.dot_general(keys, read(0, j, 1), NT, preferred_element_type=F32),
                lax.dot_general(values, read(1, j, 1), NT, preferred_element_type=F32),
            )

        ahead = dots(0)
        for j in range(heads):
            s_all, dp_all = ahead
            if j + 1 < heads:
                ahead = dots(j + 1)
            top = total = dot = None
            for b in range(blocks):
                rows = slice(b * toks, (b + 1) * toks)
                s = (s_all[rows] + bias_ref[chunk, rows, :]).reshape(toks // 8, 8, toks)
                dp = dp_all[rows].reshape(toks // 8, 8, toks)
                new = jnp.max(s, axis=0)
                new = new if top is None else jnp.maximum(top, new)
                e = jnp.exp2(s * TO_LOG2 - (new * TO_LOG2)[None])
                e_sum, e_dot = jnp.sum(e, axis=0), jnp.sum(e * dp, axis=0)
                if top is not None:
                    old = jnp.exp2(top * TO_LOG2 - new * TO_LOG2)
                    e_sum, e_dot = old * total + e_sum, old * dot + e_dot
                top, total, dot = new, e_sum, e_dot
            most = jnp.max(top, axis=0, keepdims=True)
            weight = jnp.exp2((top - most) * TO_LOG2)
            stat_ref[0, h, chunk, j : j + 1, :] = most * TO_LOG2
            stat_ref[1, h, chunk, j : j + 1, :] = jnp.sum(total * weight, axis=0, keepdims=True)
            stat_ref[2, h, chunk, j : j + 1, :] = jnp.sum(dot * weight, axis=0, keepdims=True)


def prefix_kernel(mine_ref, others_ref, pref_ref, slot_ref, stat_ref, full_ref, out_ref):
    count, _, each, _ = pref_ref.shape
    found, heads = units(mine_ref, others_ref)
    slots = count * each // PLEN
    grads = {}
    for h, chunk, read in found:
        if not chunk:
            columns = slice(h * HD, (h + 1) * HD)
            keys, values = (
                jnp.concatenate(
                    [pref_ref[part, which, :, columns].astype(F32) for part in range(count)], axis=0
                ).astype(BF16)
                for which in range(2)
            )
        q, g = read(0, 0, heads), read(1, 0, heads)
        slot = jnp.concatenate([slot_ref[chunk]] * heads, axis=1)
        s_all = lax.dot_general(keys, q, NT, preferred_element_type=F32)
        dp_all = lax.dot_general(values, g, NT, preferred_element_type=F32)
        s, dp = s_all[:PLEN], dp_all[:PLEN]
        for k in range(1, slots):
            rows = slice(k * PLEN, (k + 1) * PLEN)
            s = jnp.where(slot == k, s_all[rows], s)
            dp = jnp.where(slot == k, dp_all[rows], dp)
        top = joined(stat_ref, 0, h, chunk)
        new = jnp.maximum(top, jnp.max(s, axis=0, keepdims=True) * TO_LOG2)
        e = jnp.exp2(s * TO_LOG2 - new)
        old = jnp.exp2(top - new)
        total = old * joined(stat_ref, 1, h, chunk) + jnp.sum(e, axis=0, keepdims=True)
        dot = old * joined(stat_ref, 2, h, chunk) + jnp.sum(e * dp, axis=0, keepdims=True)
        inverse = 1.0 / total
        delta = dot * inverse
        p = e * inverse
        ds = p * (dp - delta)
        split(full_ref, 0, h, chunk, new + jnp.log2(total))
        split(full_ref, 1, h, chunk, delta)
        zero = jnp.zeros_like(p)

        def spread(x, slot=slot, zero=zero):
            return jnp.concatenate(
                [jnp.where(slot == k, x, zero).astype(BF16) for k in range(slots)], axis=0
            )

        grads[chunk] = (
            lax.dot_general(spread(ds), q, NN, preferred_element_type=F32),
            lax.dot_general(spread(p), g, NN, preferred_element_type=F32),
        )
        if chunk:
            dk, dv = (grads[0][0] + grads[1][0]) * SCALE, grads[0][1] + grads[1][1]
            for which, grad in enumerate((dk, dv)):
                for part in range(count):
                    rows = grad[part * each : (part + 1) * each]
                    out_ref[2 * which + h, part] = rows.astype(BF16)


def token_grads_kernel(core_ref, mine_ref, others_ref, *refs):
    window, (bias_ref, full_ref, home_ref, one_ref, two_ref) = refs[:4], refs[4:]
    core = core_ref[0]
    even = core == 0
    toks = mine_ref.shape[1]
    found, heads = units(mine_ref, others_ref)
    grads = {}
    for h, chunk, read in found:
        keys, values = (windows(core, h, which, *window)[chunk] for which in range(2))
        q, g = read(0, 0, heads), read(1, 0, heads)
        bias = jnp.concatenate([bias_ref[chunk]] * heads, axis=1)
        s = lax.dot_general(keys, q, NT, preferred_element_type=F32) + bias
        dp = lax.dot_general(values, g, NT, preferred_element_type=F32)
        p = jnp.exp2(s * TO_LOG2 - joined(full_ref, 0, h, chunk))
        ds = (p * (dp - joined(full_ref, 1, h, chunk))).astype(BF16)
        dk = lax.dot_general(ds, q, NN, preferred_element_type=F32) * SCALE
        dv = lax.dot_general(p.astype(BF16), g, NN, preferred_element_type=F32)
        grads[chunk] = (dk, dv)
        if not chunk:
            continue
        columns = slice(h * HD, (h + 1) * HD)
        for which in range(2):
            a, b = (
                [grads[c][which][n * toks : (n + 1) * toks] for n in range(5)] for c in range(2)
            )
            zero = jnp.zeros_like(a[4])
            home_ref[which, :toks, columns] = a[0] + jnp.where(even, b[4], zero)
            home_ref[which, toks:, columns] = b[0] + jnp.where(even, zero, a[4])
            one_ref[which, :toks, columns] = (a[1] + b[1]).astype(BF16)
            one_ref[which, toks:, columns] = (a[3] + b[2]).astype(BF16)
            two_ref[which, :toks, columns] = (a[2] + jnp.where(even, zero, b[4])).astype(BF16)
            two_ref[which, toks:, columns] = (b[3] + jnp.where(even, a[4], zero)).astype(BF16)


def halves_kernel(core_ref, q_ref, g_ref, mine_ref, theirs_ref, sems):
    width = mine_ref.shape[2]
    copies = []
    for which, ref in enumerate((q_ref, g_ref)):
        for n, (out, side) in enumerate(((theirs_ref, 1 - core_ref[0]), (mine_ref, core_ref[0]))):
            columns = pl.ds(pl.multiple_of(side * width, HD), width)
            copies.append(
                pltpu.make_async_copy(ref.at[:, columns], out.at[which], sems.at[which, n])
            )
    for copy in copies:
        copy.start()
    for copy in copies:
        copy.wait()


def halves(cores, q, g):
    half = jax.ShapeDtypeStruct((2, q.shape[0], q.shape[1] // 2), q.dtype)
    anywhere = pl.BlockSpec(memory_space=pl.ANY)
    return pl.pallas_call(
        halves_kernel,
        in_specs=[pl.BlockSpec(memory_space=pltpu.SMEM), anywhere, anywhere],
        out_specs=[pl.BlockSpec(memory_space=pltpu.VMEM), anywhere],
        out_shape=[half, half],
        scratch_shapes=[pltpu.SemaphoreType.DMA((2, 2))],
        cost_estimate=pl.CostEstimate(flops=0, bytes_accessed=4 * q.size * 2, transcendentals=0),
    )(cores, q, g)


def spread_kernel(got_ref, out_ref):
    count, cores = out_ref.shape[:2]
    for c in range(cores):
        total = got_ref[c].astype(F32)
        for n in range(c + cores, got_ref.shape[0], cores):
            total = total + got_ref[n].astype(F32)
        total = total.astype(BF16)
        for n in range(count):
            out_ref[n, c] = total


def finish_kernel(got_ref, keys_ref, values_ref):
    heads, cores = got_ref.shape[2:4]
    for which, out_ref in enumerate((keys_ref, values_ref)):
        for h in range(heads):
            for c in range(cores):
                total = got_ref[0, which, h, c].astype(F32)
                for y in range(1, got_ref.shape[0]):
                    total = total + got_ref[y, which, h, c].astype(F32)
                at = (c * heads + h) * HD
                out_ref[:, at : at + HD] = total


def call(kernel, flops, exps, ins, outs):
    space = pl.BlockSpec(memory_space=pltpu.VMEM)
    scalar = pl.BlockSpec(memory_space=pltpu.SMEM)
    return pl.pallas_call(
        kernel,
        in_specs=[scalar if x.ndim == 1 else space for x in ins],
        out_specs=[space] * len(outs),
        out_shape=outs,
        compiler_params=pltpu.CompilerParams(vmem_limit_bytes=VMEM_BYTES),
        cost_estimate=pl.CostEstimate(flops=flops, bytes_accessed=6 << 20, transcendentals=exps),
    )(*ins)


def layout(lengths, tenants, slots, block, shards, toks):
    ends = jnp.cumsum(lengths)
    slot_of = jnp.sum(
        jnp.where(tenants[:, None] == jnp.arange(slots.shape[0])[None, :], slots[None, :], 0), axis=1
    )
    here = block * toks + jnp.arange(toks, dtype=jnp.int32)
    doc = jnp.sum((here[None, :] >= ends[:, None]).astype(jnp.int32), axis=0)
    pick = doc[None, :] == jnp.arange(lengths.shape[0])[:, None]
    first = jnp.sum(jnp.where(pick, (ends - lengths)[:, None], 0), axis=0)
    slot = jnp.sum(jnp.where(pick, slot_of[:, None], 0), axis=0)
    key = jnp.concatenate([s * toks + jnp.arange(toks, dtype=jnp.int32) for s in shards])
    ok = (key[:, None] >= first[None, :]) & (key[:, None] <= here[None, :])
    return jnp.where(ok, 0.0, -1e30).astype(F32), slot[None, :].astype(jnp.int32)


def per_device(
    queries, keys, values, grad_out, prefix_keys, prefix_values, doc_lengths, doc_tenants, tenant_slots
):
    toks, width = queries.shape
    parts = lax.axis_size("z")
    count = parts * 2
    index, core = lax.axis_index(SEQ), lax.axis_index("core").astype(jnp.int32)
    even = core == 0
    cores = core[None]

    def shift(x, steps):
        pairs = [(i, i + 2 * steps) for i in range(count) if 0 <= i + 2 * steps < count]
        return lax.ppermute(x, SEQ, pairs)

    def swap(x):
        return lax.ppermute(x, SEQ, [(i, i ^ 1) for i in range(count)])

    def exchange(x, axis):
        return lax.all_to_all(x, axis, split_axis=0, concat_axis=0, tiled=True)

    def other_half(x):
        size = x.shape[-1] // 2
        return lax.dynamic_slice_in_dim(x, (1 - core) * size, size, x.ndim - 1)

    own = jnp.stack([keys, values])
    one, two = shift(own, 1), shift(own, 2)
    pref = jnp.stack([prefix_keys, prefix_values])
    pref = pref.reshape(2, -1, 2, KVH * HD // 2).transpose(2, 0, 1, 3)
    pref = jnp.broadcast_to(pref[None], (parts, *pref.shape)).reshape(count, *pref.shape[1:])
    pref = exchange(pref, SEQ)
    mine, theirs = halves(cores, queries, grad_out)
    others = swap(theirs)
    cross = swap(jnp.stack([other_half(own), other_half(one), other_half(two)]))

    facing = index ^ 1
    near, far = jnp.where(even, index - 1, index - 3), jnp.where(even, index - 3, index - 1)
    docs = (doc_lengths[0], doc_tenants[0], tenant_slots)
    shards = [index, index - 2, index - 4, near, far]
    bias0, slot0 = layout(*docs, index, shards, toks)
    last = jnp.where(even, index, index - 4)
    shards = [facing, index - 2, facing - 2, facing - 4, last]
    bias1, slot1 = layout(*docs, facing, shards, toks)
    bias, slot = jnp.stack([bias0, bias1]), jnp.stack([slot0, slot1])

    heads = [mine, others]
    shape = (KVH // 2, 2, HQ // KVH, toks)
    work = queries.size // HD * bias.shape[1]
    window = [cores, *heads, own, one, two, cross, bias]
    (stats,) = call(
        token_stats_kernel,
        flops=4 * HD * work,
        exps=work,
        ins=window,
        outs=[jax.ShapeDtypeStruct((3, *shape), F32)],
    )
    prefs = queries.size // HD * count * pref.shape[2]
    full, rows = call(
        prefix_kernel,
        flops=8 * HD * prefs,
        exps=prefs // 6,
        ins=[*heads, pref, slot, stats],
        outs=[
            jax.ShapeDtypeStruct((2, *shape), F32),
            jax.ShapeDtypeStruct((KVH, count, pref.shape[2], HD), BF16),
        ],
    )
    wide = (2, 2 * toks, KVH * HD // 2)
    home, back1, back2 = call(
        token_grads_kernel,
        flops=8 * HD * work,
        exps=work,
        ins=window + [full],
        outs=[jax.ShapeDtypeStruct(wide, kind) for kind in (F32, BF16, BF16)],
    )

    rows = exchange(rows.reshape(-1, *rows.shape[2:]), ("x", *SEQ))
    spread = jax.ShapeDtypeStruct((lax.axis_size(DP), 2, *rows.shape[1:]), BF16)
    (rows,) = call(spread_kernel, flops=rows.size, exps=0, ins=[rows], outs=[spread])
    rows, home, _, _ = lax.optimization_barrier((rows, home, back1, back2))
    rows = exchange(rows, DP).reshape(lax.axis_size("y"), 2, 2, *rows.shape[1:])
    full = jax.ShapeDtypeStruct((prefix_keys.shape[0], KVH * HD), F32)
    pref_key_grads, pref_value_grads = call(
        finish_kernel, flops=rows.size, exps=0, ins=[rows], outs=[full, full]
    )

    back1, back2 = shift(back1, -1), shift(back2, -2)
    grads = (home + back1.astype(F32) + back2.astype(F32)).astype(BF16)
    mine, theirs = grads[:, :toks], swap(grads[:, toks:])
    grads = jnp.concatenate(
        [jnp.where(even, mine, theirs), jnp.where(even, theirs, mine)], axis=2
    )
    return grads[0], grads[1], pref_key_grads, pref_value_grads


def solution(mesh):
    mesh = Mesh(mesh.devices.reshape(8, 4, 8, 2), ("y", "x", "z", "core"))
    rows, dp, seq = P(("y", "x", "z", "core"), None), P(DP, None), P(SEQ, None)
    return jax.shard_map(
        per_device,
        mesh=mesh,
        in_specs=(rows, rows, rows, rows, seq, seq, dp, dp, P()),
        out_specs=(rows, rows, seq, seq),
        check_vma=False,
    )
```

```python
import math

import jax
import jax.numpy as jnp
from jax import lax
from jax.experimental import pallas as pl
from jax.experimental.pallas import tpu as pltpu
from jax.sharding import Mesh, PartitionSpec as P

HQ = 48
KVH = 4
HD = 128
PLEN = 64
NT = (((1,), (1,)), ((), ()))
NN = (((1,), (0,)), ((), ()))
SEQ = ("z", "core")
DP = ("y", "x")
SCALE = 1.0 / math.sqrt(HD)
TO_LOG2 = SCALE * math.log2(math.e)
F32 = jnp.float32
BF16 = jnp.bfloat16


def heads_of(ref, start, count, lead=()):
    columns = [slice(start + j * HD, start + (j + 1) * HD) for j in range(count)]
    return jnp.concatenate([ref[(*lead, slice(None), c)] for c in columns], axis=0)


def joined(ref, kind, h, chunk):
    return jnp.concatenate([ref[kind, h, chunk, j : j + 1, :] for j in range(ref.shape[3])], axis=1)


def split(ref, kind, h, chunk, row):
    for j in range(ref.shape[3]):
        ref[kind, h, chunk, j : j + 1, :] = row[:, j * HD : (j + 1) * HD]


def units(core, q_ref, g_ref, others_ref, rows_ref, sems):
    kept = KVH // 2
    run = q_ref.shape[1] // KVH
    copies, found = {}, []
    for h in range(kept):
        for chunk in range(2):
            for which, ref in enumerate((q_ref, g_ref)):
                start = h * run if chunk else pl.multiple_of((core * kept + h) * run, HD)
                source = others_ref.at[which] if chunk else ref
                copies[h, chunk, which] = pltpu.make_async_copy(
                    source.at[:, pl.ds(start, run)],
                    rows_ref.at[h, chunk, which],
                    sems.at[h, chunk, which],
                )
    for copy in copies.values():
        copy.start()
    for h in range(kept):
        for chunk in range(2):

            def ready(h=h, chunk=chunk):
                copies[h, chunk, 0].wait()
                copies[h, chunk, 1].wait()

            def read(which, first, count, h=h, chunk=chunk):
                return heads_of(rows_ref, first * HD, count, (h, chunk, which))

            found.append((h, chunk, ready, read))
    return found, run // HD


def windows(core, h, which, own_ref, one_ref, two_ref, cross_ref):
    at = pl.ds(pl.multiple_of((core * (KVH // 2) + h) * HD, HD), HD)
    own, one, two = (ref[which, :, at] for ref in (own_ref, one_ref, two_ref))
    cross = [cross_ref[n, which, :, h * HD : (h + 1) * HD] for n in range(3)]
    even = core == 0
    last = jnp.where(even, own.astype(F32), two.astype(F32)).astype(BF16)
    far = jnp.where(even, cross[2].astype(F32), cross[0].astype(F32)).astype(BF16)
    return (
        jnp.concatenate([own, one, two, cross[1], far], axis=0),
        jnp.concatenate([cross[0], one, cross[1], cross[2], last], axis=0),
    )


def token_stats_kernel(core_ref, q_ref, g_ref, others_ref, *refs):
    window, (bias_ref, stat_ref, rows_ref, sems) = refs[:4], refs[4:]
    core = core_ref[0]
    toks = q_ref.shape[0]
    blocks = bias_ref.shape[1] // toks
    found, heads = units(core, q_ref, g_ref, others_ref, rows_ref, sems)
    for h, chunk, ready, read in found:
        keys, values = (windows(core, h, which, *window)[chunk] for which in range(2))

        ready()

        def dots(j, keys=keys, values=values, read=read):
            return (
                lax.dot_general(keys, read(0, j, 1), NT, preferred_element_type=F32),
                lax.dot_general(values, read(1, j, 1), NT, preferred_element_type=F32),
            )

        ahead = dots(0)
        for j in range(heads):
            s_all, dp_all = ahead
            if j + 1 < heads:
                ahead = dots(j + 1)
            top = total = dot = None
            for b in range(blocks):
                rows = slice(b * toks, (b + 1) * toks)
                s = (s_all[rows] + bias_ref[chunk, rows, :]).reshape(toks // 8, 8, toks)
                dp = dp_all[rows].reshape(toks // 8, 8, toks)
                new = jnp.max(s, axis=0)
                new = new if top is None else jnp.maximum(top, new)
                e = jnp.exp2(s * TO_LOG2 - (new * TO_LOG2)[None])
                e_sum, e_dot = jnp.sum(e, axis=0), jnp.sum(e * dp, axis=0)
                if top is not None:
                    old = jnp.exp2(top * TO_LOG2 - new * TO_LOG2)
                    e_sum, e_dot = old * total + e_sum, old * dot + e_dot
                top, total, dot = new, e_sum, e_dot
            most = jnp.max(top, axis=0, keepdims=True)
            weight = jnp.exp2((top - most) * TO_LOG2)
            stat_ref[0, h, chunk, j : j + 1, :] = most * TO_LOG2
            stat_ref[1, h, chunk, j : j + 1, :] = jnp.sum(total * weight, axis=0, keepdims=True)
            stat_ref[2, h, chunk, j : j + 1, :] = jnp.sum(dot * weight, axis=0, keepdims=True)


def prefix_kernel(
    core_ref, q_ref, g_ref, others_ref, pref_ref, slot_ref, stat_ref, full_ref, out_ref, rows_ref, sems
):
    count, _, each, _ = pref_ref.shape
    found, heads = units(core_ref[0], q_ref, g_ref, others_ref, rows_ref, sems)
    slots = count * each // PLEN
    grads = {}
    for h, chunk, ready, read in found:
        if not chunk:
            columns = slice(h * HD, (h + 1) * HD)
            keys, values = (
                jnp.concatenate(
                    [pref_ref[part, which, :, columns].astype(F32) for part in range(count)], axis=0
                ).astype(BF16)
                for which in range(2)
            )
        ready()
        q, g = read(0, 0, heads), read(1, 0, heads)
        slot = jnp.concatenate([slot_ref[chunk]] * heads, axis=1)
        s_all = lax.dot_general(keys, q, NT, preferred_element_type=F32)
        dp_all = lax.dot_general(values, g, NT, preferred_element_type=F32)
        s, dp = s_all[:PLEN], dp_all[:PLEN]
        for k in range(1, slots):
            rows = slice(k * PLEN, (k + 1) * PLEN)
            s = jnp.where(slot == k, s_all[rows], s)
            dp = jnp.where(slot == k, dp_all[rows], dp)
        top = joined(stat_ref, 0, h, chunk)
        new = jnp.maximum(top, jnp.max(s, axis=0, keepdims=True) * TO_LOG2)
        e = jnp.exp2(s * TO_LOG2 - new)
        old = jnp.exp2(top - new)
        total = old * joined(stat_ref, 1, h, chunk) + jnp.sum(e, axis=0, keepdims=True)
        dot = old * joined(stat_ref, 2, h, chunk) + jnp.sum(e * dp, axis=0, keepdims=True)
        inverse = 1.0 / total
        delta = dot * inverse
        p = e * inverse
        ds = p * (dp - delta)
        split(full_ref, 0, h, chunk, new + jnp.log2(total))
        split(full_ref, 1, h, chunk, delta)
        zero = jnp.zeros_like(p)

        def spread(x, slot=slot, zero=zero):
            return jnp.concatenate(
                [jnp.where(slot == k, x, zero).astype(BF16) for k in range(slots)], axis=0
            )

        grads[chunk] = (
            lax.dot_general(spread(ds), q, NN, preferred_element_type=F32),
            lax.dot_general(spread(p), g, NN, preferred_element_type=F32),
        )
        if chunk:
            dk, dv = (grads[0][0] + grads[1][0]) * SCALE, grads[0][1] + grads[1][1]
            for which, grad in enumerate((dk, dv)):
                for part in range(count):
                    rows = grad[part * each : (part + 1) * each]
                    out_ref[2 * which + h, part] = rows.astype(BF16)


def token_grads_kernel(core_ref, q_ref, g_ref, others_ref, *refs):
    window, (bias_ref, full_ref, home_ref, one_ref, two_ref, rows_ref, sems) = refs[:4], refs[4:]
    core = core_ref[0]
    even = core == 0
    toks = q_ref.shape[0]
    found, heads = units(core, q_ref, g_ref, others_ref, rows_ref, sems)
    grads = {}
    for h, chunk, ready, read in found:
        ready()
        keys, values = (windows(core, h, which, *window)[chunk] for which in range(2))
        q, g = read(0, 0, heads), read(1, 0, heads)
        bias = jnp.concatenate([bias_ref[chunk]] * heads, axis=1)
        s = lax.dot_general(keys, q, NT, preferred_element_type=F32) + bias
        dp = lax.dot_general(values, g, NT, preferred_element_type=F32)
        p = jnp.exp2(s * TO_LOG2 - joined(full_ref, 0, h, chunk))
        ds = (p * (dp - joined(full_ref, 1, h, chunk))).astype(BF16)
        dk = lax.dot_general(ds, q, NN, preferred_element_type=F32) * SCALE
        dv = lax.dot_general(p.astype(BF16), g, NN, preferred_element_type=F32)
        grads[chunk] = (dk, dv)
        if not chunk:
            continue
        columns = slice(h * HD, (h + 1) * HD)
        for which in range(2):
            a, b = (
                [grads[c][which][n * toks : (n + 1) * toks] for n in range(5)] for c in range(2)
            )
            zero = jnp.zeros_like(a[4])
            home_ref[which, :toks, columns] = a[0] + jnp.where(even, b[4], zero)
            home_ref[which, toks:, columns] = b[0] + jnp.where(even, zero, a[4])
            one_ref[which, :toks, columns] = (a[1] + b[1]).astype(BF16)
            one_ref[which, toks:, columns] = (a[3] + b[2]).astype(BF16)
            two_ref[which, :toks, columns] = (a[2] + jnp.where(even, zero, b[4])).astype(BF16)
            two_ref[which, toks:, columns] = (b[3] + jnp.where(even, a[4], zero)).astype(BF16)


def spread_kernel(got_ref, out_ref):
    count, cores = out_ref.shape[:2]
    for c in range(cores):
        total = got_ref[c].astype(F32)
        for n in range(c + cores, got_ref.shape[0], cores):
            total = total + got_ref[n].astype(F32)
        total = total.astype(BF16)
        for n in range(count):
            out_ref[n, c] = total


def finish_kernel(got_ref, keys_ref, values_ref):
    heads, cores = got_ref.shape[2:4]
    for which, out_ref in enumerate((keys_ref, values_ref)):
        for h in range(heads):
            for c in range(cores):
                total = got_ref[0, which, h, c].astype(F32)
                for y in range(1, got_ref.shape[0]):
                    total = total + got_ref[y, which, h, c].astype(F32)
                at = (c * heads + h) * HD
                out_ref[:, at : at + HD] = total


def call(kernel, flops, exps, ins, outs, rows=()):
    space = pl.BlockSpec(memory_space=pltpu.VMEM)
    specs = [space] * len(ins)
    scratch = []
    if rows:
        far = pl.BlockSpec(memory_space=pl.ANY)
        specs = [pl.BlockSpec(memory_space=pltpu.SMEM)] + [far] * 3 + specs
        toks, width = rows[1].shape
        lead = (KVH // 2, 2, 2)
        scratch = [
            pltpu.VMEM((*lead, toks, width // KVH), BF16),
            pltpu.SemaphoreType.DMA(lead),
        ]
    return pl.pallas_call(
        kernel,
        in_specs=specs,
        out_specs=[space] * len(outs),
        out_shape=outs,
        scratch_shapes=scratch,
        compiler_params=pltpu.CompilerParams(vmem_limit_bytes=(60 if rows else 16) << 20),
        cost_estimate=pl.CostEstimate(flops=flops, bytes_accessed=6 << 20, transcendentals=exps),
    )(*rows, *ins)


def layout(lengths, tenants, slots, block, shards, toks):
    ends = jnp.cumsum(lengths)
    slot_of = jnp.sum(
        jnp.where(tenants[:, None] == jnp.arange(slots.shape[0])[None, :], slots[None, :], 0), axis=1
    )
    here = block * toks + jnp.arange(toks, dtype=jnp.int32)
    doc = jnp.sum((here[None, :] >= ends[:, None]).astype(jnp.int32), axis=0)
    pick = doc[None, :] == jnp.arange(lengths.shape[0])[:, None]
    first = jnp.sum(jnp.where(pick, (ends - lengths)[:, None], 0), axis=0)
    slot = jnp.sum(jnp.where(pick, slot_of[:, None], 0), axis=0)
    key = jnp.concatenate([s * toks + jnp.arange(toks, dtype=jnp.int32) for s in shards])
    ok = (key[:, None] >= first[None, :]) & (key[:, None] <= here[None, :])
    return jnp.where(ok, 0.0, -1e30).astype(F32), slot[None, :].astype(jnp.int32)


def per_device(
    queries, keys, values, grad_out, prefix_keys, prefix_values, doc_lengths, doc_tenants, tenant_slots
):
    toks, width = queries.shape
    parts = lax.axis_size("z")
    count = parts * 2
    index, core = lax.axis_index(SEQ), lax.axis_index("core").astype(jnp.int32)
    even = core == 0
    cores = core[None]

    def shift(x, steps):
        pairs = [(i, i + 2 * steps) for i in range(count) if 0 <= i + 2 * steps < count]
        return lax.ppermute(x, SEQ, pairs)

    def swap(x):
        return lax.ppermute(x, SEQ, [(i, i ^ 1) for i in range(count)])

    def exchange(x, axis):
        return lax.all_to_all(x, axis, split_axis=0, concat_axis=0, tiled=True)

    def other_half(x):
        size = x.shape[-1] // 2
        return lax.dynamic_slice_in_dim(x, (1 - core) * size, size, x.ndim - 1)

    own = jnp.stack([keys, values])
    one, two = shift(own, 1), shift(own, 2)
    pref = jnp.stack([prefix_keys, prefix_values])
    pref = pref.reshape(2, -1, 2, KVH * HD // 2).transpose(2, 0, 1, 3)
    pref = jnp.broadcast_to(pref[None], (parts, *pref.shape)).reshape(count, *pref.shape[1:])
    pref = exchange(pref, SEQ)
    others = swap(jnp.stack([other_half(queries), other_half(grad_out)]))
    cross = swap(jnp.stack([other_half(own), other_half(one), other_half(two)]))

    facing = index ^ 1
    near, far = jnp.where(even, index - 1, index - 3), jnp.where(even, index - 3, index - 1)
    docs = (doc_lengths[0], doc_tenants[0], tenant_slots)
    shards = [index, index - 2, index - 4, near, far]
    bias0, slot0 = layout(*docs, index, shards, toks)
    last = jnp.where(even, index, index - 4)
    shards = [facing, index - 2, facing - 2, facing - 4, last]
    bias1, slot1 = layout(*docs, facing, shards, toks)
    bias, slot = jnp.stack([bias0, bias1]), jnp.stack([slot0, slot1])

    rows_in = (cores, queries, grad_out, others)
    shape = (KVH // 2, 2, HQ // KVH, toks)
    work = queries.size // HD * bias.shape[1]
    window = [own, one, two, cross, bias]
    (stats,) = call(
        token_stats_kernel,
        flops=4 * HD * work,
        exps=work,
        ins=window,
        outs=[jax.ShapeDtypeStruct((3, *shape), F32)],
        rows=rows_in,
    )
    prefs = queries.size // HD * count * pref.shape[2]
    full, rows = call(
        prefix_kernel,
        flops=8 * HD * prefs,
        exps=prefs // 6,
        ins=[pref, slot, stats],
        rows=rows_in,
        outs=[
            jax.ShapeDtypeStruct((2, *shape), F32),
            jax.ShapeDtypeStruct((KVH, count, pref.shape[2], HD), BF16),
        ],
    )
    wide = (2, 2 * toks, KVH * HD // 2)
    home, back1, back2 = call(
        token_grads_kernel,
        flops=8 * HD * work,
        exps=work,
        ins=window + [full],
        rows=rows_in,
        outs=[jax.ShapeDtypeStruct(wide, kind) for kind in (F32, BF16, BF16)],
    )

    rows = exchange(rows.reshape(-1, *rows.shape[2:]), ("x", *SEQ))
    spread = jax.ShapeDtypeStruct((lax.axis_size(DP), 2, *rows.shape[1:]), BF16)
    (rows,) = call(spread_kernel, flops=rows.size, exps=0, ins=[rows], outs=[spread])
    rows, home, _, _ = lax.optimization_barrier((rows, home, back1, back2))
    rows = exchange(rows, DP).reshape(lax.axis_size("y"), 2, 2, *rows.shape[1:])
    full = jax.ShapeDtypeStruct((prefix_keys.shape[0], KVH * HD), F32)
    pref_key_grads, pref_value_grads = call(
        finish_kernel, flops=rows.size, exps=0, ins=[rows], outs=[full, full]
    )

    back1, back2 = shift(back1, -1), shift(back2, -2)
    grads = (home + back1.astype(F32) + back2.astype(F32)).astype(BF16)
    mine, theirs = grads[:, :toks], swap(grads[:, toks:])
    grads = jnp.concatenate(
        [jnp.where(even, mine, theirs), jnp.where(even, theirs, mine)], axis=2
    )
    return grads[0], grads[1], pref_key_grads, pref_value_grads


def solution(mesh):
    mesh = Mesh(mesh.devices.reshape(8, 4, 8, 2), ("y", "x", "z", "core"))
    rows, dp, seq = P(("y", "x", "z", "core"), None), P(DP, None), P(SEQ, None)
    return jax.shard_map(
        per_device,
        mesh=mesh,
        in_specs=(rows, rows, rows, rows, seq, seq, dp, dp, P()),
        out_specs=(rows, rows, seq, seq),
        check_vma=False,
    )
```

```python
import math

import jax
import jax.numpy as jnp
from jax import lax
from jax.experimental import pallas as pl
from jax.experimental.pallas import tpu as pltpu
from jax.sharding import Mesh, PartitionSpec as P

HQ = 48
KVH = 4
HD = 128
PLEN = 64
NT = (((1,), (1,)), ((), ()))
NN = (((1,), (0,)), ((), ()))
SEQ = ("z", "core")
DP = ("y", "x")
SCALE = 1.0 / math.sqrt(HD)
TO_LOG2 = SCALE * math.log2(math.e)
F32 = jnp.float32
BF16 = jnp.bfloat16
VMEM_BYTES = 20 << 20


def heads_of(ref, start, count, lead=()):
    columns = [slice(start + j * HD, start + (j + 1) * HD) for j in range(count)]
    return jnp.concatenate([ref[(*lead, slice(None), c)] for c in columns], axis=0)


def joined(ref, kind, h, chunk):
    return jnp.concatenate([ref[kind, h, chunk, j : j + 1, :] for j in range(ref.shape[3])], axis=1)


def split(ref, kind, h, chunk, row):
    for j in range(ref.shape[3]):
        ref[kind, h, chunk, j : j + 1, :] = row[:, j * HD : (j + 1) * HD]


def units(mine_ref, others_ref):
    kept = KVH // 2
    run = mine_ref.shape[2] // kept
    found = []
    for h in range(kept):
        for chunk, ref in enumerate((mine_ref, others_ref)):

            def read(which, first, count, h=h, ref=ref):
                return heads_of(ref, h * run + first * HD, count, (which,))

            found.append((h, chunk, read))
    return found, run // HD


def windows(core, h, which, own_ref, one_ref, two_ref, cross_ref):
    at = pl.ds(pl.multiple_of((core * (KVH // 2) + h) * HD, HD), HD)
    own, one, two = (ref[which, :, at] for ref in (own_ref, one_ref, two_ref))
    cross = [cross_ref[n, which, :, h * HD : (h + 1) * HD] for n in range(3)]
    even = core == 0
    last = jnp.where(even, own.astype(F32), two.astype(F32)).astype(BF16)
    far = jnp.where(even, cross[2].astype(F32), cross[0].astype(F32)).astype(BF16)
    return (
        jnp.concatenate([own, one, two, cross[1], far], axis=0),
        jnp.concatenate([cross[0], one, cross[1], cross[2], last], axis=0),
    )


def masks(where_ref, first_ref, toks):
    down = lax.broadcasted_iota(jnp.int32, (toks, toks), 0)
    along = lax.broadcasted_iota(jnp.int32, (toks, toks), 1)
    found = []
    for chunk in range(2):
        at = 1 + chunk * 6
        here = along + where_ref[at] * toks
        found.append([])
        for b in range(5):
            key = down + where_ref[at + 1 + b] * toks
            seen = (key >= first_ref[chunk]) & (key <= here)
            found[-1].append(jnp.where(seen, 0.0, -1e30).astype(F32))
    return found


def token_stats_kernel(where_ref, mine_ref, others_ref, *refs):
    window, (first_ref, stat_ref) = refs[:4], refs[4:]
    core = where_ref[0]
    toks = mine_ref.shape[1]
    hidden = masks(where_ref, first_ref, toks)
    blocks = len(hidden[0])
    found, heads = units(mine_ref, others_ref)
    for h, chunk, read in found:
        keys, values = (windows(core, h, which, *window)[chunk] for which in range(2))

        def dots(j, keys=keys, values=values, read=read):
            return (
                lax.dot_general(keys, read(0, j, 1), NT, preferred_element_type=F32),
                lax.dot_general(values, read(1, j, 1), NT, preferred_element_type=F32),
            )

        ahead = dots(0)
        for j in range(heads):
            s_all, dp_all = ahead
            if j + 1 < heads:
                ahead = dots(j + 1)
            top = total = dot = None
            for b in range(blocks):
                rows = slice(b * toks, (b + 1) * toks)
                s = (s_all[rows] + hidden[chunk][b]).reshape(toks // 8, 8, toks)
                dp = dp_all[rows].reshape(toks // 8, 8, toks)
                new = jnp.max(s, axis=0)
                new = new if top is None else jnp.maximum(top, new)
                e = jnp.exp2(s * TO_LOG2 - (new * TO_LOG2)[None])
                e_sum, e_dot = jnp.sum(e, axis=0), jnp.sum(e * dp, axis=0)
                if top is not None:
                    old = jnp.exp2(top * TO_LOG2 - new * TO_LOG2)
                    e_sum, e_dot = old * total + e_sum, old * dot + e_dot
                top, total, dot = new, e_sum, e_dot
            most = jnp.max(top, axis=0, keepdims=True)
            weight = jnp.exp2((top - most) * TO_LOG2)
            stat_ref[0, h, chunk, j : j + 1, :] = most * TO_LOG2
            stat_ref[1, h, chunk, j : j + 1, :] = jnp.sum(total * weight, axis=0, keepdims=True)
            stat_ref[2, h, chunk, j : j + 1, :] = jnp.sum(dot * weight, axis=0, keepdims=True)


def prefix_kernel(mine_ref, others_ref, pref_ref, slot_ref, stat_ref, full_ref, out_ref):
    count, _, each, _ = pref_ref.shape
    found, heads = units(mine_ref, others_ref)
    slots = count * each // PLEN
    grads = {}
    for h, chunk, read in found:
        if not chunk:
            columns = slice(h * HD, (h + 1) * HD)
            keys, values = (
                jnp.concatenate(
                    [pref_ref[part, which, :, columns].astype(F32) for part in range(count)], axis=0
                ).astype(BF16)
                for which in range(2)
            )
        q, g = read(0, 0, heads), read(1, 0, heads)
        slot = jnp.concatenate([slot_ref[chunk]] * heads, axis=1)
        s_all = lax.dot_general(keys, q, NT, preferred_element_type=F32)
        dp_all = lax.dot_general(values, g, NT, preferred_element_type=F32)
        s, dp = s_all[:PLEN], dp_all[:PLEN]
        for k in range(1, slots):
            rows = slice(k * PLEN, (k + 1) * PLEN)
            s = jnp.where(slot == k, s_all[rows], s)
            dp = jnp.where(slot == k, dp_all[rows], dp)
        top = joined(stat_ref, 0, h, chunk)
        new = jnp.maximum(top, jnp.max(s, axis=0, keepdims=True) * TO_LOG2)
        e = jnp.exp2(s * TO_LOG2 - new)
        old = jnp.exp2(top - new)
        total = old * joined(stat_ref, 1, h, chunk) + jnp.sum(e, axis=0, keepdims=True)
        dot = old * joined(stat_ref, 2, h, chunk) + jnp.sum(e * dp, axis=0, keepdims=True)
        inverse = 1.0 / total
        delta = dot * inverse
        p = e * inverse
        ds = p * (dp - delta)
        split(full_ref, 0, h, chunk, new + jnp.log2(total))
        split(full_ref, 1, h, chunk, delta)
        zero = jnp.zeros_like(p)

        def spread(x, slot=slot, zero=zero):
            return jnp.concatenate(
                [jnp.where(slot == k, x, zero).astype(BF16) for k in range(slots)], axis=0
            )

        grads[chunk] = (
            lax.dot_general(spread(ds), q, NN, preferred_element_type=F32),
            lax.dot_general(spread(p), g, NN, preferred_element_type=F32),
        )
        if chunk:
            dk, dv = (grads[0][0] + grads[1][0]) * SCALE, grads[0][1] + grads[1][1]
            for which, grad in enumerate((dk, dv)):
                for part in range(count):
                    rows = grad[part * each : (part + 1) * each]
                    out_ref[2 * which + h, part] = rows.astype(BF16)


def token_grads_kernel(where_ref, mine_ref, others_ref, *refs):
    window, (first_ref, full_ref, home_ref, one_ref, two_ref) = refs[:4], refs[4:]
    core = where_ref[0]
    even = core == 0
    toks = mine_ref.shape[1]
    hidden = masks(where_ref, first_ref, toks)
    found, heads = units(mine_ref, others_ref)
    grads = {}
    for h, chunk, read in found:
        keys, values = (windows(core, h, which, *window)[chunk] for which in range(2))
        q, g = read(0, 0, heads), read(1, 0, heads)
        bias = jnp.concatenate([jnp.concatenate(hidden[chunk], axis=0)] * heads, axis=1)
        s = lax.dot_general(keys, q, NT, preferred_element_type=F32) + bias
        dp = lax.dot_general(values, g, NT, preferred_element_type=F32)
        p = jnp.exp2(s * TO_LOG2 - joined(full_ref, 0, h, chunk))
        ds = (p * (dp - joined(full_ref, 1, h, chunk))).astype(BF16)
        dk = lax.dot_general(ds, q, NN, preferred_element_type=F32) * SCALE
        dv = lax.dot_general(p.astype(BF16), g, NN, preferred_element_type=F32)
        grads[chunk] = (dk, dv)
        if not chunk:
            continue
        columns = slice(h * HD, (h + 1) * HD)
        for which in range(2):
            a, b = (
                [grads[c][which][n * toks : (n + 1) * toks] for n in range(5)] for c in range(2)
            )
            zero = jnp.zeros_like(a[4])
            home_ref[which, :toks, columns] = a[0] + jnp.where(even, b[4], zero)
            home_ref[which, toks:, columns] = b[0] + jnp.where(even, zero, a[4])
            one_ref[which, :toks, columns] = (a[1] + b[1]).astype(BF16)
            one_ref[which, toks:, columns] = (a[3] + b[2]).astype(BF16)
            two_ref[which, :toks, columns] = (a[2] + jnp.where(even, zero, b[4])).astype(BF16)
            two_ref[which, toks:, columns] = (b[3] + jnp.where(even, a[4], zero)).astype(BF16)


def spread_kernel(got_ref, out_ref):
    count, cores = out_ref.shape[:2]
    for c in range(cores):
        total = got_ref[c].astype(F32)
        for n in range(c + cores, got_ref.shape[0], cores):
            total = total + got_ref[n].astype(F32)
        total = total.astype(BF16)
        for n in range(count):
            out_ref[n, c] = total


def finish_kernel(got_ref, keys_ref, values_ref):
    heads, cores = got_ref.shape[2:4]
    for which, out_ref in enumerate((keys_ref, values_ref)):
        for h in range(heads):
            for c in range(cores):
                total = got_ref[0, which, h, c].astype(F32)
                for y in range(1, got_ref.shape[0]):
                    total = total + got_ref[y, which, h, c].astype(F32)
                at = (c * heads + h) * HD
                out_ref[:, at : at + HD] = total


def call(kernel, flops, exps, ins, outs):
    space = pl.BlockSpec(memory_space=pltpu.VMEM)
    scalar = pl.BlockSpec(memory_space=pltpu.SMEM)
    return pl.pallas_call(
        kernel,
        in_specs=[scalar if x.ndim == 1 else space for x in ins],
        out_specs=[space] * len(outs),
        out_shape=outs,
        compiler_params=pltpu.CompilerParams(vmem_limit_bytes=VMEM_BYTES),
        cost_estimate=pl.CostEstimate(flops=flops, bytes_accessed=6 << 20, transcendentals=exps),
    )(*ins)


def layout(lengths, tenants, slots, block, toks):
    ends = jnp.cumsum(lengths)
    slot_of = jnp.sum(
        jnp.where(tenants[:, None] == jnp.arange(slots.shape[0])[None, :], slots[None, :], 0), axis=1
    )
    here = block * toks + jnp.arange(toks, dtype=jnp.int32)
    doc = jnp.sum((here[None, :] >= ends[:, None]).astype(jnp.int32), axis=0)
    pick = doc[None, :] == jnp.arange(lengths.shape[0])[:, None]
    first = jnp.sum(jnp.where(pick, (ends - lengths)[:, None], 0), axis=0)
    slot = jnp.sum(jnp.where(pick, slot_of[:, None], 0), axis=0)
    return first[None, :].astype(jnp.int32), slot[None, :].astype(jnp.int32)


def per_device(
    queries, keys, values, grad_out, prefix_keys, prefix_values, doc_lengths, doc_tenants, tenant_slots
):
    toks, width = queries.shape
    parts = lax.axis_size("z")
    count = parts * 2
    index, core = lax.axis_index(SEQ), lax.axis_index("core").astype(jnp.int32)
    even = core == 0

    def shift(x, steps):
        pairs = [(i, i + 2 * steps) for i in range(count) if 0 <= i + 2 * steps < count]
        return lax.ppermute(x, SEQ, pairs)

    def swap(x):
        return lax.ppermute(x, SEQ, [(i, i ^ 1) for i in range(count)])

    def exchange(x, axis):
        return lax.all_to_all(x, axis, split_axis=0, concat_axis=0, tiled=True)

    def half(x, which):
        size = x.shape[-1] // 2
        return lax.dynamic_slice_in_dim(x, which * size, size, x.ndim - 1)

    own = jnp.stack([keys, values])
    one, two = shift(own, 1), shift(own, 2)
    pref = jnp.stack([prefix_keys, prefix_values])
    pref = pref.reshape(2, -1, 2, KVH * HD // 2).transpose(2, 0, 1, 3)
    pref = jnp.broadcast_to(pref[None], (parts, *pref.shape)).reshape(count, *pref.shape[1:])
    pref = exchange(pref, SEQ)
    others = swap(jnp.stack([half(queries, 1 - core), half(grad_out, 1 - core)]))
    cross = swap(jnp.stack([half(x, 1 - core) for x in (own, one, two)]))

    facing = index ^ 1
    near, far = jnp.where(even, index - 1, index - 3), jnp.where(even, index - 3, index - 1)
    docs = (doc_lengths[0], doc_tenants[0], tenant_slots)
    first0, slot0 = layout(*docs, index, toks)
    first1, slot1 = layout(*docs, facing, toks)
    first, slot = jnp.stack([first0, first1]), jnp.stack([slot0, slot1])
    last = jnp.where(even, index, index - 4)
    where = [core, index, index, index - 2, index - 4, near, far]
    where += [facing, facing, index - 2, facing - 2, facing - 4, last]
    where = jnp.stack(where).astype(jnp.int32)

    heads = [jnp.stack([half(queries, core), half(grad_out, core)]), others]
    shape = (KVH // 2, 2, HQ // KVH, toks)
    work = queries.size // HD * 5 * toks
    window = [where, *heads, own, one, two, cross, first]
    (stats,) = call(
        token_stats_kernel,
        flops=4 * HD * work,
        exps=work,
        ins=window,
        outs=[jax.ShapeDtypeStruct((3, *shape), F32)],
    )
    prefs = queries.size // HD * count * pref.shape[2]
    full, rows = call(
        prefix_kernel,
        flops=8 * HD * prefs,
        exps=prefs // 6,
        ins=[*heads, pref, slot, stats],
        outs=[
            jax.ShapeDtypeStruct((2, *shape), F32),
            jax.ShapeDtypeStruct((KVH, count, pref.shape[2], HD), BF16),
        ],
    )
    wide = (2, 2 * toks, KVH * HD // 2)
    home, back1, back2 = call(
        token_grads_kernel,
        flops=8 * HD * work,
        exps=work,
        ins=window + [full],
        outs=[jax.ShapeDtypeStruct(wide, kind) for kind in (F32, BF16, BF16)],
    )

    back1, back2 = shift(back1, -1), shift(back2, -2)

    rows = exchange(rows.reshape(-1, *rows.shape[2:]), ("x", *SEQ))
    spread = jax.ShapeDtypeStruct((lax.axis_size(DP), 2, *rows.shape[1:]), BF16)
    (rows,) = call(spread_kernel, flops=rows.size, exps=0, ins=[rows], outs=[spread])
    rows, home = lax.optimization_barrier((rows, home))
    rows = exchange(rows, DP).reshape(lax.axis_size("y"), 2, 2, *rows.shape[1:])
    full = jax.ShapeDtypeStruct((prefix_keys.shape[0], KVH * HD), F32)
    pref_key_grads, pref_value_grads = call(
        finish_kernel, flops=rows.size, exps=0, ins=[rows], outs=[full, full]
    )

    grads = (home + back1.astype(F32) + back2.astype(F32)).astype(BF16)
    mine, theirs = grads[:, :toks], swap(grads[:, toks:])
    grads = jnp.concatenate(
        [jnp.where(even, mine, theirs), jnp.where(even, theirs, mine)], axis=2
    )
    return grads[0], grads[1], pref_key_grads, pref_value_grads


def solution(mesh):
    mesh = Mesh(mesh.devices.reshape(8, 4, 8, 2), ("y", "x", "z", "core"))
    rows, dp, seq = P(("y", "x", "z", "core"), None), P(DP, None), P(SEQ, None)
    return jax.shard_map(
        per_device,
        mesh=mesh,
        in_specs=(rows, rows, rows, rows, seq, seq, dp, dp, P()),
        out_specs=(rows, rows, seq, seq),
        check_vma=False,
    )
```

```python
import math

import jax
import jax.numpy as jnp
from jax import lax
from jax.experimental import pallas as pl
from jax.experimental.pallas import tpu as pltpu
from jax.sharding import Mesh, PartitionSpec as P

HQ = 48
KVH = 4
HD = 128
PLEN = 64
NT = (((1,), (1,)), ((), ()))
NN = (((1,), (0,)), ((), ()))
SEQ = ("z", "core")
DP = ("y", "x")
SCALE = 1.0 / math.sqrt(HD)
TO_LOG2 = SCALE * math.log2(math.e)
F32 = jnp.float32
BF16 = jnp.bfloat16
SHORT = 4
VMEM_BYTES = 20 << 20


def heads_of(ref, start, count, lead=()):
    columns = [slice(start + j * HD, start + (j + 1) * HD) for j in range(count)]
    return jnp.concatenate([ref[(*lead, slice(None), c)] for c in columns], axis=0)


def joined(ref, kind, h, chunk):
    return jnp.concatenate([ref[kind, h, chunk, j : j + 1, :] for j in range(ref.shape[3])], axis=1)


def split(ref, kind, h, chunk, row):
    for j in range(ref.shape[3]):
        ref[kind, h, chunk, j : j + 1, :] = row[:, j * HD : (j + 1) * HD]


def units(q_ref, g_ref, others_ref):
    kept = KVH // 2
    run = q_ref.shape[1] // kept
    found = []
    for h in range(kept):
        for chunk in range(2):

            def read(which, first, count, h=h, chunk=chunk):
                start = h * run + first * HD
                if chunk:
                    return heads_of(others_ref, start, count, (which,))
                return heads_of(g_ref if which else q_ref, start, count)

            found.append((h, chunk, read))
    return found, run // HD


def windows(core, h, which, own_ref, one_ref, two_ref, cross_ref):
    at = pl.ds(pl.multiple_of((core * (KVH // 2) + h) * HD, HD), HD)
    own, one, two = (ref[which, :, at] for ref in (own_ref, one_ref, two_ref))
    cross = [cross_ref[n, which, :, h * HD : (h + 1) * HD] for n in range(3)]
    even = core == 0
    last = jnp.where(even, own.astype(F32), two.astype(F32)).astype(BF16)
    far = jnp.where(even, cross[2].astype(F32), cross[0].astype(F32)).astype(BF16)
    return (
        jnp.concatenate([own, one, two, cross[1], far], axis=0),
        jnp.concatenate([cross[0], one, cross[1], cross[2], last], axis=0),
    )


def tokens(chunk, toks, where_ref, lengths_ref, tenants_ref, slots_ref):
    core, index = where_ref[0], where_ref[1]
    begin = (index + chunk * (1 - 2 * core)) * toks
    here = lax.broadcasted_iota(jnp.int32, (1, toks), 1) + begin
    docs = lengths_ref.shape[1]
    doc = first = slot = jnp.zeros((1, toks), jnp.int32)
    start, low, high = jnp.int32(0), jnp.int32(-1), jnp.int32(-1)
    for n in range(docs):
        reached = here >= start
        doc = jnp.where(reached, n, doc)
        first = jnp.where(reached, start, first)
        slot = jnp.where(reached, slots_ref[tenants_ref[0, n]], slot)
        low = low + (begin >= start).astype(jnp.int32)
        high = high + (begin + toks - 1 >= start).astype(jnp.int32)
        start = start + lengths_ref[0, n]
    some = [slots_ref[tenants_ref[0, jnp.minimum(low + n, docs - 1)]] for n in range(SHORT)]
    return here, first, slot, doc - low, high - low + 1, some


def masks(toks, *where_refs):
    core, index = where_refs[0][0], where_refs[0][1]
    even = core == 0
    facing = index + 1 - 2 * core
    near, far = jnp.where(even, index - 1, index - 3), jnp.where(even, index - 3, index - 1)
    last = jnp.where(even, index, index - 4)
    shards = (
        (index, index - 2, index - 4, near, far),
        (facing, index - 2, facing - 2, facing - 4, last),
    )
    down = lax.broadcasted_iota(jnp.int32, (toks, toks), 0)
    found = []
    for chunk in range(2):
        here, first = tokens(chunk, toks, *where_refs)[:2]
        found.append([])
        for shard in shards[chunk]:
            key = down + shard * toks
            seen = (key >= first) & (key <= here)
            found[-1].append(jnp.where(seen, 0.0, -1e30).astype(F32))
    return found


def token_stats_kernel(where_ref, lengths_ref, tenants_ref, slots_ref, q_ref, g_ref, others_ref, *refs):
    window, (stat_ref,) = refs[:4], refs[4:]
    core = where_ref[0]
    toks = q_ref.shape[0]
    hidden = masks(toks, where_ref, lengths_ref, tenants_ref, slots_ref)
    blocks = len(hidden[0])
    found, heads = units(q_ref, g_ref, others_ref)
    for h, chunk, read in found:
        keys, values = (windows(core, h, which, *window)[chunk] for which in range(2))

        def dots(j, keys=keys, values=values, read=read):
            return (
                lax.dot_general(keys, read(0, j, 1), NT, preferred_element_type=F32),
                lax.dot_general(values, read(1, j, 1), NT, preferred_element_type=F32),
            )

        ahead = dots(0)
        for j in range(heads):
            s_all, dp_all = ahead
            if j + 1 < heads:
                ahead = dots(j + 1)
            top = total = dot = None
            for b in range(blocks):
                rows = slice(b * toks, (b + 1) * toks)
                s = (s_all[rows] + hidden[chunk][b]).reshape(toks // 8, 8, toks)
                dp = dp_all[rows].reshape(toks // 8, 8, toks)
                new = jnp.max(s, axis=0)
                new = new if top is None else jnp.maximum(top, new)
                e = jnp.exp2(s * TO_LOG2 - (new * TO_LOG2)[None])
                e_sum, e_dot = jnp.sum(e, axis=0), jnp.sum(e * dp, axis=0)
                if top is not None:
                    old = jnp.exp2(top * TO_LOG2 - new * TO_LOG2)
                    e_sum, e_dot = old * total + e_sum, old * dot + e_dot
                top, total, dot = new, e_sum, e_dot
            most = jnp.max(top, axis=0, keepdims=True)
            weight = jnp.exp2((top - most) * TO_LOG2)
            stat_ref[0, h, chunk, j : j + 1, :] = most * TO_LOG2
            stat_ref[1, h, chunk, j : j + 1, :] = jnp.sum(total * weight, axis=0, keepdims=True)
            stat_ref[2, h, chunk, j : j + 1, :] = jnp.sum(dot * weight, axis=0, keepdims=True)


def prefix_kernel(
    where_ref, lengths_ref, tenants_ref, slots_ref, q_ref, g_ref, others_ref, pref_ref, stat_ref,
    full_ref, out_ref, rows_ref, sum_ref,
):
    count, _, each, _ = pref_ref.shape
    found, heads = units(q_ref, g_ref, others_ref)
    slots = count * each // PLEN
    found_docs = [
        tokens(chunk, q_ref.shape[0], where_ref, lengths_ref, tenants_ref, slots_ref)
        for chunk in range(2)
    ]
    for which in range(2):
        for h in range(KVH // 2):
            parts = [pref_ref[n, which, :, h * HD : (h + 1) * HD].astype(F32) for n in range(count)]
            rows_ref[which, h] = jnp.concatenate(parts, axis=0).astype(BF16)

    def form(short):
        for h, chunk, read in found:
            _, _, slot, place, _, some = found_docs[chunk]
            if short:
                places = [pl.ds(pl.multiple_of(n * PLEN, PLEN), PLEN) for n in some]
            else:
                places = [slice(k * PLEN, (k + 1) * PLEN) for k in range(slots)]
            keys, values = (
                jnp.concatenate([rows_ref[which, h, p] for p in places], axis=0)
                for which in range(2)
            )
            q, g = read(0, 0, heads), read(1, 0, heads)
            place = jnp.concatenate([place if short else slot] * heads, axis=1)
            s_all = lax.dot_general(keys, q, NT, preferred_element_type=F32)
            dp_all = lax.dot_general(values, g, NT, preferred_element_type=F32)
            s, dp = s_all[:PLEN], dp_all[:PLEN]
            for k in range(1, len(places)):
                rows = slice(k * PLEN, (k + 1) * PLEN)
                s = jnp.where(place == k, s_all[rows], s)
                dp = jnp.where(place == k, dp_all[rows], dp)
            top = joined(stat_ref, 0, h, chunk)
            new = jnp.maximum(top, jnp.max(s, axis=0, keepdims=True) * TO_LOG2)
            e = jnp.exp2(s * TO_LOG2 - new)
            old = jnp.exp2(top - new)
            total = old * joined(stat_ref, 1, h, chunk) + jnp.sum(e, axis=0, keepdims=True)
            dot = old * joined(stat_ref, 2, h, chunk) + jnp.sum(e * dp, axis=0, keepdims=True)
            inverse = 1.0 / total
            delta = dot * inverse
            p = e * inverse
            ds = p * (dp - delta)
            split(full_ref, 0, h, chunk, new + jnp.log2(total))
            split(full_ref, 1, h, chunk, delta)
            zero = jnp.zeros_like(p)

            def spread(x, place=place, zero=zero, places=places):
                return jnp.concatenate(
                    [jnp.where(place == k, x, zero).astype(BF16) for k in range(len(places))], axis=0
                )

            grads = (
                lax.dot_general(spread(ds), q, NN, preferred_element_type=F32) * SCALE,
                lax.dot_general(spread(p), g, NN, preferred_element_type=F32),
            )
            if not chunk:
                sum_ref[...] = jnp.zeros_like(sum_ref)
            for which, grad in enumerate(grads):
                for k, p in enumerate(places):
                    sum_ref[which, p] += grad[k * PLEN : (k + 1) * PLEN]
                if chunk:
                    for part in range(count):
                        rows = sum_ref[which, part * each : (part + 1) * each]
                        out_ref[2 * which + h, part] = rows.astype(BF16)

    few = jnp.maximum(found_docs[0][4], found_docs[1][4]) <= SHORT
    pl.when(few)(lambda: form(True))
    pl.when(jnp.logical_not(few))(lambda: form(False))


def token_grads_kernel(where_ref, lengths_ref, tenants_ref, slots_ref, q_ref, g_ref, others_ref, *refs):
    window, (full_ref, home_ref, one_ref, two_ref) = refs[:4], refs[4:]
    core = where_ref[0]
    even = core == 0
    toks = q_ref.shape[0]
    hidden = masks(toks, where_ref, lengths_ref, tenants_ref, slots_ref)
    found, heads = units(q_ref, g_ref, others_ref)
    grads = {}
    for h, chunk, read in found:
        keys, values = (windows(core, h, which, *window)[chunk] for which in range(2))
        q, g = read(0, 0, heads), read(1, 0, heads)
        bias = jnp.concatenate([jnp.concatenate(hidden[chunk], axis=0)] * heads, axis=1)
        s = lax.dot_general(keys, q, NT, preferred_element_type=F32) + bias
        dp = lax.dot_general(values, g, NT, preferred_element_type=F32)
        p = jnp.exp2(s * TO_LOG2 - joined(full_ref, 0, h, chunk))
        ds = (p * (dp - joined(full_ref, 1, h, chunk))).astype(BF16)
        dk = lax.dot_general(ds, q, NN, preferred_element_type=F32) * SCALE
        dv = lax.dot_general(p.astype(BF16), g, NN, preferred_element_type=F32)
        grads[chunk] = (dk, dv)
        if not chunk:
            continue
        columns = slice(h * HD, (h + 1) * HD)
        for which in range(2):
            a, b = (
                [grads[c][which][n * toks : (n + 1) * toks] for n in range(5)] for c in range(2)
            )
            zero = jnp.zeros_like(a[4])
            home_ref[which, :toks, columns] = a[0] + jnp.where(even, b[4], zero)
            home_ref[which, toks:, columns] = b[0] + jnp.where(even, zero, a[4])
            one_ref[which, :toks, columns] = (a[1] + b[1]).astype(BF16)
            one_ref[which, toks:, columns] = (a[3] + b[2]).astype(BF16)
            two_ref[which, :toks, columns] = (a[2] + jnp.where(even, zero, b[4])).astype(BF16)
            two_ref[which, toks:, columns] = (b[3] + jnp.where(even, a[4], zero)).astype(BF16)


def spread_kernel(got_ref, out_ref):
    count, cores = out_ref.shape[:2]
    for c in range(cores):
        total = got_ref[c].astype(F32)
        for n in range(c + cores, got_ref.shape[0], cores):
            total = total + got_ref[n].astype(F32)
        total = total.astype(BF16)
        for n in range(count):
            out_ref[n, c] = total


def finish_kernel(got_ref, keys_ref, values_ref):
    heads, cores = got_ref.shape[2:4]
    for which, out_ref in enumerate((keys_ref, values_ref)):
        for h in range(heads):
            for c in range(cores):
                total = got_ref[0, which, h, c].astype(F32)
                for y in range(1, got_ref.shape[0]):
                    total = total + got_ref[y, which, h, c].astype(F32)
                at = (c * heads + h) * HD
                out_ref[:, at : at + HD] = total


def call(kernel, flops, exps, ins, outs, scratch=()):
    space = pl.BlockSpec(memory_space=pltpu.VMEM)
    scalars = pl.BlockSpec(memory_space=pltpu.SMEM)
    return pl.pallas_call(
        kernel,
        in_specs=[scalars if x.dtype == jnp.int32 else space for x in ins],
        out_specs=[space] * len(outs),
        out_shape=outs,
        scratch_shapes=scratch,
        compiler_params=pltpu.CompilerParams(vmem_limit_bytes=VMEM_BYTES),
        cost_estimate=pl.CostEstimate(flops=flops, bytes_accessed=6 << 20, transcendentals=exps),
    )(*ins)


def per_device(
    queries, keys, values, grad_out, prefix_keys, prefix_values, doc_lengths, doc_tenants, tenant_slots
):
    toks, width = queries.shape
    parts = lax.axis_size("z")
    count = parts * 2
    index, core = lax.axis_index(SEQ), lax.axis_index("core").astype(jnp.int32)
    even = core == 0

    def shift(x, steps):
        pairs = [(i, i + 2 * steps) for i in range(count) if 0 <= i + 2 * steps < count]
        return lax.ppermute(x, SEQ, pairs)

    def swap(x):
        return lax.ppermute(x, SEQ, [(i, i ^ 1) for i in range(count)])

    def exchange(x, axis):
        return lax.all_to_all(x, axis, split_axis=0, concat_axis=0, tiled=True)

    def half(x, which):
        size = x.shape[-1] // 2
        return lax.dynamic_slice_in_dim(x, which * size, size, x.ndim - 1)

    own = jnp.stack([keys, values])
    one, two = shift(own, 1), shift(own, 2)
    pref = jnp.stack([prefix_keys, prefix_values])
    pref = pref.reshape(2, -1, 2, KVH * HD // 2).transpose(2, 0, 1, 3)
    pref = jnp.broadcast_to(pref[None], (parts, *pref.shape)).reshape(count, *pref.shape[1:])
    pref = exchange(pref, SEQ)
    others = swap(jnp.stack([half(queries, 1 - core), half(grad_out, 1 - core)]))
    cross = swap(jnp.stack([half(x, 1 - core) for x in (own, one, two)]))

    where = (jnp.stack([core, index.astype(jnp.int32)]), doc_lengths, doc_tenants, tenant_slots)
    heads = [half(queries, core), half(grad_out, core), others]
    shape = (KVH // 2, 2, HQ // KVH, toks)
    work = queries.size // HD * 5 * toks
    window = [*where, *heads, own, one, two, cross]
    (stats,) = call(
        token_stats_kernel,
        flops=4 * HD * work,
        exps=work,
        ins=window,
        outs=[jax.ShapeDtypeStruct((3, *shape), F32)],
    )
    prefs = queries.size // HD * count * pref.shape[2]
    full, rows = call(
        prefix_kernel,
        flops=8 * HD * prefs,
        exps=prefs // 6,
        ins=[*where, *heads, pref, stats],
        scratch=[
            pltpu.VMEM((2, KVH // 2, count * pref.shape[2], HD), BF16),
            pltpu.VMEM((2, count * pref.shape[2], HD), F32),
        ],
        outs=[
            jax.ShapeDtypeStruct((2, *shape), F32),
            jax.ShapeDtypeStruct((KVH, count, pref.shape[2], HD), BF16),
        ],
    )
    wide = (2, 2 * toks, KVH * HD // 2)
    home, back1, back2 = call(
        token_grads_kernel,
        flops=8 * HD * work,
        exps=work,
        ins=window + [full],
        outs=[jax.ShapeDtypeStruct(wide, kind) for kind in (F32, BF16, BF16)],
    )

    back1, back2 = shift(back1, -1), shift(back2, -2)

    rows = exchange(rows.reshape(-1, *rows.shape[2:]), ("x", *SEQ))
    spread = jax.ShapeDtypeStruct((lax.axis_size(DP), 2, *rows.shape[1:]), BF16)
    (rows,) = call(spread_kernel, flops=rows.size, exps=0, ins=[rows], outs=[spread])
    rows, home = lax.optimization_barrier((rows, home))
    rows = exchange(rows, DP).reshape(lax.axis_size("y"), 2, 2, *rows.shape[1:])
    full = jax.ShapeDtypeStruct((prefix_keys.shape[0], KVH * HD), F32)
    pref_key_grads, pref_value_grads = call(
        finish_kernel, flops=rows.size, exps=0, ins=[rows], outs=[full, full]
    )

    grads = (home + back1.astype(F32) + back2.astype(F32)).astype(BF16)
    mine, theirs = grads[:, :toks], swap(grads[:, toks:])
    grads = jnp.concatenate(
        [jnp.where(even, mine, theirs), jnp.where(even, theirs, mine)], axis=2
    )
    return grads[0], grads[1], pref_key_grads, pref_value_grads


def solution(mesh):
    mesh = Mesh(mesh.devices.reshape(8, 4, 8, 2), ("y", "x", "z", "core"))
    rows, dp, seq = P(("y", "x", "z", "core"), None), P(DP, None), P(SEQ, None)
    return jax.shard_map(
        per_device,
        mesh=mesh,
        in_specs=(rows, rows, rows, rows, seq, seq, dp, dp, P()),
        out_specs=(rows, rows, seq, seq),
        check_vma=False,
    )
```

```python
import math

import jax
import jax.numpy as jnp
from jax import lax
from jax.experimental import pallas as pl
from jax.experimental.pallas import tpu as pltpu
from jax.sharding import Mesh, PartitionSpec as P

HQ = 48
KVH = 4
HD = 128
PLEN = 64
NT = (((1,), (1,)), ((), ()))
NN = (((1,), (0,)), ((), ()))
SEQ = ("z", "core")
DP = ("y", "x")
SCALE = 1.0 / math.sqrt(HD)
TO_LOG2 = SCALE * math.log2(math.e)
F32 = jnp.float32
BF16 = jnp.bfloat16
SHORT = 4
VMEM_BYTES = 20 << 20


def heads_of(ref, start, count, lead=()):
    columns = [slice(start + j * HD, start + (j + 1) * HD) for j in range(count)]
    return jnp.concatenate([ref[(*lead, slice(None), c)] for c in columns], axis=0)


def joined(ref, kind, h, chunk):
    return jnp.concatenate([ref[kind, h, chunk, j : j + 1, :] for j in range(ref.shape[3])], axis=1)


def split(ref, kind, h, chunk, row):
    for j in range(ref.shape[3]):
        ref[kind, h, chunk, j : j + 1, :] = row[:, j * HD : (j + 1) * HD]


def units(mine_ref, others_ref):
    kept = KVH // 2
    run = mine_ref.shape[2] // kept
    found = []
    for h in range(kept):
        for chunk, ref in enumerate((mine_ref, others_ref)):

            def read(which, first, count, h=h, ref=ref):
                return heads_of(ref, h * run + first * HD, count, (which,))

            found.append((h, chunk, read))
    return found, run // HD


def windows(core, h, which, own_ref, one_ref, two_ref, cross_ref):
    at = pl.ds(pl.multiple_of((core * (KVH // 2) + h) * HD, HD), HD)
    own, one, two = (ref[which, :, at] for ref in (own_ref, one_ref, two_ref))
    cross = [cross_ref[n, which, :, h * HD : (h + 1) * HD] for n in range(3)]
    even = core == 0
    last = jnp.where(even, own.astype(F32), two.astype(F32)).astype(BF16)
    far = jnp.where(even, cross[2].astype(F32), cross[0].astype(F32)).astype(BF16)
    return (
        jnp.concatenate([own, one, two, cross[1], far], axis=0),
        jnp.concatenate([cross[0], one, cross[1], cross[2], last], axis=0),
    )


def tokens(chunk, toks, where_ref, lengths_ref, tenants_ref, slots_ref):
    core, index = where_ref[0], where_ref[1]
    begin = (index + chunk * (1 - 2 * core)) * toks
    here = lax.broadcasted_iota(jnp.int32, (1, toks), 1) + begin
    docs = lengths_ref.shape[1]
    doc = first = slot = jnp.zeros((1, toks), jnp.int32)
    start, low, high = jnp.int32(0), jnp.int32(-1), jnp.int32(-1)
    for n in range(docs):
        reached = here >= start
        doc = jnp.where(reached, n, doc)
        first = jnp.where(reached, start, first)
        slot = jnp.where(reached, slots_ref[tenants_ref[0, n]], slot)
        low = low + (begin >= start).astype(jnp.int32)
        high = high + (begin + toks - 1 >= start).astype(jnp.int32)
        start = start + lengths_ref[0, n]
    some = [slots_ref[tenants_ref[0, jnp.minimum(low + n, docs - 1)]] for n in range(SHORT)]
    return here, first, slot, doc - low, high - low + 1, some


def masks(where_ref, first_ref, toks):
    down = lax.broadcasted_iota(jnp.int32, (toks, toks), 0)
    along = lax.broadcasted_iota(jnp.int32, (toks, toks), 1)
    found = []
    for chunk in range(2):
        at = 1 + chunk * 6
        here = along + where_ref[at] * toks
        found.append([])
        for b in range(5):
            key = down + where_ref[at + 1 + b] * toks
            seen = (key >= first_ref[chunk]) & (key <= here)
            found[-1].append(jnp.where(seen, 0.0, -1e30).astype(F32))
    return found


def token_stats_kernel(where_ref, mine_ref, others_ref, *refs):
    window, (first_ref, stat_ref) = refs[:4], refs[4:]
    core = where_ref[0]
    toks = mine_ref.shape[1]
    hidden = masks(where_ref, first_ref, toks)
    blocks = len(hidden[0])
    found, heads = units(mine_ref, others_ref)
    for h, chunk, read in found:
        keys, values = (windows(core, h, which, *window)[chunk] for which in range(2))

        def dots(j, keys=keys, values=values, read=read):
            return (
                lax.dot_general(keys, read(0, j, 1), NT, preferred_element_type=F32),
                lax.dot_general(values, read(1, j, 1), NT, preferred_element_type=F32),
            )

        ahead = dots(0)
        for j in range(heads):
            s_all, dp_all = ahead
            if j + 1 < heads:
                ahead = dots(j + 1)
            top = total = dot = None
            for b in range(blocks):
                rows = slice(b * toks, (b + 1) * toks)
                s = (s_all[rows] + hidden[chunk][b]).reshape(toks // 8, 8, toks)
                dp = dp_all[rows].reshape(toks // 8, 8, toks)
                new = jnp.max(s, axis=0)
                new = new if top is None else jnp.maximum(top, new)
                e = jnp.exp2(s * TO_LOG2 - (new * TO_LOG2)[None])
                e_sum, e_dot = jnp.sum(e, axis=0), jnp.sum(e * dp, axis=0)
                if top is not None:
                    old = jnp.exp2(top * TO_LOG2 - new * TO_LOG2)
                    e_sum, e_dot = old * total + e_sum, old * dot + e_dot
                top, total, dot = new, e_sum, e_dot
            most = jnp.max(top, axis=0, keepdims=True)
            weight = jnp.exp2((top - most) * TO_LOG2)
            stat_ref[0, h, chunk, j : j + 1, :] = most * TO_LOG2
            stat_ref[1, h, chunk, j : j + 1, :] = jnp.sum(total * weight, axis=0, keepdims=True)
            stat_ref[2, h, chunk, j : j + 1, :] = jnp.sum(dot * weight, axis=0, keepdims=True)


def prefix_kernel(
    where_ref, lengths_ref, tenants_ref, slots_ref, mine_ref, others_ref, pref_ref, stat_ref,
    full_ref, out_ref, rows_ref, sum_ref,
):
    count, _, each, _ = pref_ref.shape
    found, heads = units(mine_ref, others_ref)
    slots = count * each // PLEN
    found_docs = [
        tokens(chunk, mine_ref.shape[1], where_ref, lengths_ref, tenants_ref, slots_ref)
        for chunk in range(2)
    ]
    for which in range(2):
        for h in range(KVH // 2):
            parts = [pref_ref[n, which, :, h * HD : (h + 1) * HD].astype(F32) for n in range(count)]
            rows_ref[which, h] = jnp.concatenate(parts, axis=0).astype(BF16)

    def form(short):
        for h, chunk, read in found:
            _, _, slot, place, _, some = found_docs[chunk]
            if short:
                places = [pl.ds(pl.multiple_of(n * PLEN, PLEN), PLEN) for n in some]
            else:
                places = [slice(k * PLEN, (k + 1) * PLEN) for k in range(slots)]
            keys, values = (
                jnp.concatenate([rows_ref[which, h, p] for p in places], axis=0)
                for which in range(2)
            )
            q, g = read(0, 0, heads), read(1, 0, heads)
            place = jnp.concatenate([place if short else slot] * heads, axis=1)
            s_all = lax.dot_general(keys, q, NT, preferred_element_type=F32)
            dp_all = lax.dot_general(values, g, NT, preferred_element_type=F32)
            s, dp = s_all[:PLEN], dp_all[:PLEN]
            for k in range(1, len(places)):
                rows = slice(k * PLEN, (k + 1) * PLEN)
                s = jnp.where(place == k, s_all[rows], s)
                dp = jnp.where(place == k, dp_all[rows], dp)
            top = joined(stat_ref, 0, h, chunk)
            new = jnp.maximum(top, jnp.max(s, axis=0, keepdims=True) * TO_LOG2)
            e = jnp.exp2(s * TO_LOG2 - new)
            old = jnp.exp2(top - new)
            total = old * joined(stat_ref, 1, h, chunk) + jnp.sum(e, axis=0, keepdims=True)
            dot = old * joined(stat_ref, 2, h, chunk) + jnp.sum(e * dp, axis=0, keepdims=True)
            inverse = 1.0 / total
            delta = dot * inverse
            p = e * inverse
            ds = p * (dp - delta)
            split(full_ref, 0, h, chunk, new + jnp.log2(total))
            split(full_ref, 1, h, chunk, delta)
            zero = jnp.zeros_like(p)

            def spread(x, place=place, zero=zero, places=places):
                return jnp.concatenate(
                    [jnp.where(place == k, x, zero).astype(BF16) for k in range(len(places))], axis=0
                )

            grads = (
                lax.dot_general(spread(ds), q, NN, preferred_element_type=F32) * SCALE,
                lax.dot_general(spread(p), g, NN, preferred_element_type=F32),
            )
            if not chunk:
                sum_ref[...] = jnp.zeros_like(sum_ref)
            for which, grad in enumerate(grads):
                for k, p in enumerate(places):
                    sum_ref[which, p] += grad[k * PLEN : (k + 1) * PLEN]
                if chunk:
                    for part in range(count):
                        rows = sum_ref[which, part * each : (part + 1) * each]
                        out_ref[2 * which + h, part] = rows.astype(BF16)

    few = jnp.maximum(found_docs[0][4], found_docs[1][4]) <= SHORT
    pl.when(few)(lambda: form(True))
    pl.when(jnp.logical_not(few))(lambda: form(False))


def token_grads_kernel(where_ref, mine_ref, others_ref, *refs):
    window, (first_ref, full_ref, home_ref, one_ref, two_ref) = refs[:4], refs[4:]
    core = where_ref[0]
    even = core == 0
    toks = mine_ref.shape[1]
    hidden = masks(where_ref, first_ref, toks)
    found, heads = units(mine_ref, others_ref)
    grads = {}
    for h, chunk, read in found:
        keys, values = (windows(core, h, which, *window)[chunk] for which in range(2))
        q, g = read(0, 0, heads), read(1, 0, heads)
        bias = jnp.concatenate([jnp.concatenate(hidden[chunk], axis=0)] * heads, axis=1)
        s = lax.dot_general(keys, q, NT, preferred_element_type=F32) + bias
        dp = lax.dot_general(values, g, NT, preferred_element_type=F32)
        p = jnp.exp2(s * TO_LOG2 - joined(full_ref, 0, h, chunk))
        ds = (p * (dp - joined(full_ref, 1, h, chunk))).astype(BF16)
        dk = lax.dot_general(ds, q, NN, preferred_element_type=F32) * SCALE
        dv = lax.dot_general(p.astype(BF16), g, NN, preferred_element_type=F32)
        grads[chunk] = (dk, dv)
        if not chunk:
            continue
        columns = slice(h * HD, (h + 1) * HD)
        for which in range(2):
            a, b = (
                [grads[c][which][n * toks : (n + 1) * toks] for n in range(5)] for c in range(2)
            )
            zero = jnp.zeros_like(a[4])
            home_ref[which, :toks, columns] = a[0] + jnp.where(even, b[4], zero)
            home_ref[which, toks:, columns] = b[0] + jnp.where(even, zero, a[4])
            one_ref[which, :toks, columns] = (a[1] + b[1]).astype(BF16)
            one_ref[which, toks:, columns] = (a[3] + b[2]).astype(BF16)
            two_ref[which, :toks, columns] = (a[2] + jnp.where(even, zero, b[4])).astype(BF16)
            two_ref[which, toks:, columns] = (b[3] + jnp.where(even, a[4], zero)).astype(BF16)


def spread_kernel(got_ref, out_ref):
    count, cores = out_ref.shape[:2]
    for c in range(cores):
        total = got_ref[c].astype(F32)
        for n in range(c + cores, got_ref.shape[0], cores):
            total = total + got_ref[n].astype(F32)
        total = total.astype(BF16)
        for n in range(count):
            out_ref[n, c] = total


def finish_kernel(got_ref, keys_ref, values_ref):
    heads, cores = got_ref.shape[2:4]
    for which, out_ref in enumerate((keys_ref, values_ref)):
        for h in range(heads):
            for c in range(cores):
                total = got_ref[0, which, h, c].astype(F32)
                for y in range(1, got_ref.shape[0]):
                    total = total + got_ref[y, which, h, c].astype(F32)
                at = (c * heads + h) * HD
                out_ref[:, at : at + HD] = total


def call(kernel, flops, exps, ins, outs, scratch=(), scalar=()):
    space = pl.BlockSpec(memory_space=pltpu.VMEM)
    scalars = pl.BlockSpec(memory_space=pltpu.SMEM)
    return pl.pallas_call(
        kernel,
        in_specs=[scalars if n in scalar else space for n in range(len(ins))],
        out_specs=[space] * len(outs),
        out_shape=outs,
        scratch_shapes=scratch,
        compiler_params=pltpu.CompilerParams(vmem_limit_bytes=VMEM_BYTES),
        cost_estimate=pl.CostEstimate(flops=flops, bytes_accessed=6 << 20, transcendentals=exps),
    )(*ins)


def layout(lengths, tenants, slots, block, toks):
    ends = jnp.cumsum(lengths)
    slot_of = jnp.sum(
        jnp.where(tenants[:, None] == jnp.arange(slots.shape[0])[None, :], slots[None, :], 0), axis=1
    )
    here = block * toks + jnp.arange(toks, dtype=jnp.int32)
    doc = jnp.sum((here[None, :] >= ends[:, None]).astype(jnp.int32), axis=0)
    pick = doc[None, :] == jnp.arange(lengths.shape[0])[:, None]
    first = jnp.sum(jnp.where(pick, (ends - lengths)[:, None], 0), axis=0)
    slot = jnp.sum(jnp.where(pick, slot_of[:, None], 0), axis=0)
    return first[None, :].astype(jnp.int32), slot[None, :].astype(jnp.int32)


def per_device(
    queries, keys, values, grad_out, prefix_keys, prefix_values, doc_lengths, doc_tenants, tenant_slots
):
    toks, width = queries.shape
    parts = lax.axis_size("z")
    count = parts * 2
    index, core = lax.axis_index(SEQ), lax.axis_index("core").astype(jnp.int32)
    even = core == 0

    def shift(x, steps):
        pairs = [(i, i + 2 * steps) for i in range(count) if 0 <= i + 2 * steps < count]
        return lax.ppermute(x, SEQ, pairs)

    def swap(x):
        return lax.ppermute(x, SEQ, [(i, i ^ 1) for i in range(count)])

    def exchange(x, axis):
        return lax.all_to_all(x, axis, split_axis=0, concat_axis=0, tiled=True)

    def half(x, which):
        size = x.shape[-1] // 2
        return lax.dynamic_slice_in_dim(x, which * size, size, x.ndim - 1)

    own = jnp.stack([keys, values])
    one, two = shift(own, 1), shift(own, 2)
    pref = jnp.stack([prefix_keys, prefix_values])
    pref = pref.reshape(2, -1, 2, KVH * HD // 2).transpose(2, 0, 1, 3)
    pref = jnp.broadcast_to(pref[None], (parts, *pref.shape)).reshape(count, *pref.shape[1:])
    pref = exchange(pref, SEQ)
    others = swap(jnp.stack([half(queries, 1 - core), half(grad_out, 1 - core)]))
    cross = swap(jnp.stack([half(x, 1 - core) for x in (own, one, two)]))

    facing = index ^ 1
    near, far = jnp.where(even, index - 1, index - 3), jnp.where(even, index - 3, index - 1)
    docs = (doc_lengths[0], doc_tenants[0], tenant_slots)
    first0, slot0 = layout(*docs, index, toks)
    first1, slot1 = layout(*docs, facing, toks)
    first, slot = jnp.stack([first0, first1]), jnp.stack([slot0, slot1])
    last = jnp.where(even, index, index - 4)
    where = [core, index, index, index - 2, index - 4, near, far]
    where += [facing, facing, index - 2, facing - 2, facing - 4, last]
    where = jnp.stack(where).astype(jnp.int32)

    heads = [jnp.stack([half(queries, core), half(grad_out, core)]), others]
    shape = (KVH // 2, 2, HQ // KVH, toks)
    work = queries.size // HD * 5 * toks
    window = [where, *heads, own, one, two, cross, first]
    (stats,) = call(
        token_stats_kernel,
        flops=4 * HD * work,
        exps=work,
        ins=window,
        scalar=(0,),
        outs=[jax.ShapeDtypeStruct((3, *shape), F32)],
    )
    prefs = queries.size // HD * count * pref.shape[2]
    full, rows = call(
        prefix_kernel,
        flops=8 * HD * prefs,
        exps=prefs // 6,
        ins=[where, doc_lengths, doc_tenants, tenant_slots, *heads, pref, stats],
        scratch=[
            pltpu.VMEM((2, KVH // 2, count * pref.shape[2], HD), BF16),
            pltpu.VMEM((2, count * pref.shape[2], HD), F32),
        ],
        scalar=(0, 1, 2, 3),
        outs=[
            jax.ShapeDtypeStruct((2, *shape), F32),
            jax.ShapeDtypeStruct((KVH, count, pref.shape[2], HD), BF16),
        ],
    )
    wide = (2, 2 * toks, KVH * HD // 2)
    home, back1, back2 = call(
        token_grads_kernel,
        flops=8 * HD * work,
        exps=work,
        ins=window + [full],
        scalar=(0,),
        outs=[jax.ShapeDtypeStruct(wide, kind) for kind in (F32, BF16, BF16)],
    )

    back1, back2 = shift(back1, -1), shift(back2, -2)

    rows = exchange(rows.reshape(-1, *rows.shape[2:]), ("x", *SEQ))
    spread = jax.ShapeDtypeStruct((lax.axis_size(DP), 2, *rows.shape[1:]), BF16)
    (rows,) = call(spread_kernel, flops=rows.size, exps=0, ins=[rows], outs=[spread])
    rows, home = lax.optimization_barrier((rows, home))
    rows = exchange(rows, DP).reshape(lax.axis_size("y"), 2, 2, *rows.shape[1:])
    full = jax.ShapeDtypeStruct((prefix_keys.shape[0], KVH * HD), F32)
    pref_key_grads, pref_value_grads = call(
        finish_kernel, flops=rows.size, exps=0, ins=[rows], outs=[full, full]
    )

    grads = (home + back1.astype(F32) + back2.astype(F32)).astype(BF16)
    mine, theirs = grads[:, :toks], swap(grads[:, toks:])
    grads = jnp.concatenate(
        [jnp.where(even, mine, theirs), jnp.where(even, theirs, mine)], axis=2
    )
    return grads[0], grads[1], pref_key_grads, pref_value_grads


def solution(mesh):
    mesh = Mesh(mesh.devices.reshape(8, 4, 8, 2), ("y", "x", "z", "core"))
    rows, dp, seq = P(("y", "x", "z", "core"), None), P(DP, None), P(SEQ, None)
    return jax.shard_map(
        per_device,
        mesh=mesh,
        in_specs=(rows, rows, rows, rows, seq, seq, dp, dp, P()),
        out_specs=(rows, rows, seq, seq),
        check_vma=False,
    )
```
